32 devices in a mesh: groups: 2 (over y), ctx: 8 (over z, x), head: 2 (over core).
Axes of the slice: x: 2, y: 2, z: 4, core: 2. Of those that a mesh axis runs over, the one named last changes fastest.
Arguments:
- queries: bfloat16 [1024, 4096], P(('groups', 'ctx', 'head')), parts along dimension 0, may hold values from -6 to 6
- latents: bfloat16 [16, 64, 1280], P(('groups', 'ctx')), parts along dimension 0, may hold values from -6 to 6
- image_span: int32 [10, 2], P('groups'), parts along dimension 0, may hold values from 0 to 512, as said below
- image_owner: int32 [10], P('groups'), parts along dimension 0, may hold values from 0 to 7, as said below
- kv_weight: bfloat16 [1280, 2, 4096], P('ctx', None, 'head'), may hold values from -0.15625 to 0.15625
- attn_gate: float32 [4096], P('head'), may hold values from -1.5 to 1.5
Outputs:
- context: bfloat16 [1024, 4096], P(('groups', 'ctx', 'head')), parts along dimension 0
The draws below stay inside these ranges and needn't reach their ends.
There are 2 independent parts, one for each index of `groups`. The reference program is written for one: setup_inputs(seed, part) draws one part's arguments, and reference() takes and returns one part's arrays. A program takes and returns all parts, laid end to end along the dimension named above; an argument that names none is the same for every part. Nothing has to cross between parts.
Inputs may be any that keep to these rules, and one draw needn't show every extreme that they name: `image_span`: images are in order of position; spans are disjoint and not empty; each image starts 22 or more tokens after the previous one starts. The tokens of one ctx index, [c * 64, (c + 1) * 64), meet at most 4 spans, and some ctx index meets exactly 4. `image_owner`: owners are distinct; stores of ctx indices that own no image are not read.
All inputs are finite; a program needn't handle non-finite values.
Results may differ from the reference program's by a relative error of at most 0.0069.
Values may be sent and summed in bfloat16 or wider, within the bound.
No kernel may reach another device: no remote copies, remote signals or barrier semaphores. Data moves between devices by JAX's collectives and lax.ppermute only.
A program may use at most 64 MiB of HBM per device.

```python
import jax
import jax.numpy as jnp
from jax import lax

HEADS = 32
DH = 128
LAT = 64
LW = 1280
MAXIMG = 4
TOK_DEV = 64
TOKENS = 512
IMAGES = 5
N_CTX = 8


def draw_image_span(key, part):
    key = jax.random.fold_in(key, 11)
    keys = jax.random.split(key, 4)
    spacing = TOK_DEV // 3 + 1
    lead = (MAXIMG - 1) * spacing - TOK_DEV + 1
    rest = IMAGES - MAXIMG
    device = jax.random.randint(keys[0], (), 1, N_CTX - 1)
    block = device * TOK_DEV
    before = rest * device // (N_CTX - 1)
    after = rest - before
    index = jnp.arange(IMAGES, dtype=jnp.int32)
    length_b = block - lead
    room_b = (length_b - before * spacing) // jnp.maximum(before, 1)
    anchor_a = block - lead + MAXIMG * spacing
    length_a = TOKENS - anchor_a
    room_a = (length_a - after * spacing) // jnp.maximum(after, 1)
    raw = jax.random.randint(keys[1], (IMAGES,), 0, 1 << 20)
    keep = jax.random.randint(keys[2], (IMAGES,), 0, 3) > 0
    in_before = index < before
    in_after = index >= before + MAXIMG
    step_b = jnp.where(in_before & keep, raw % (room_b + 1), 0)
    step_a = jnp.where(in_after & keep, raw % (room_a + 1), 0)
    starts_b = index * spacing + jnp.cumsum(step_b)
    starts_c = block - lead + (index - before) * spacing
    starts_a = anchor_a + (index - before - MAXIMG) * spacing + jnp.cumsum(step_a)
    starts = jnp.where(in_before, starts_b, jnp.where(in_after, starts_a, starts_c))
    nexts = jnp.concatenate([starts[1:], jnp.full((1,), TOKENS, starts.dtype)])
    trim_raw = jax.random.randint(keys[3], (IMAGES,), 0, 1 << 20)
    trim = trim_raw % ((nexts - starts) // 2 + 1)
    tight = (index >= before) & (index < before + MAXIMG - 1)
    ends = nexts - jnp.where(tight, 0, trim)
    return jnp.stack([starts, ends], 1).astype(jnp.int32)


def draw_image_owner(key, part):
    key = jax.random.fold_in(key, 23)
    return jax.random.permutation(key, N_CTX)[:IMAGES].astype(jnp.int32)


def block_scale(rng, dims, pieces, least, top_value):
    gain = 1.0
    for position, blocks in pieces:
        draws = jax.random.uniform(jax.random.fold_in(jax.random.fold_in(rng, 6), position), (blocks,), jnp.float32, least / len(pieces), top_value / len(pieces))
        gain = gain * jnp.repeat(jnp.exp(draws), dims[position] // blocks).reshape((-1,) + (1,) * (len(dims) - 1 - position))
    return gain


def noise(rng, dims, scale, limit, pieces=(), held_as=jnp.bfloat16):
    values = scale * jax.random.normal(rng, dims, jnp.float32)
    if pieces:
        values = values * block_scale(rng, dims, pieces, -0.22, 0.18)
    return jnp.clip(values, -limit, limit).astype(held_as)


def setup_inputs(seed: int = 0, part: int = 0) -> dict:
    seeds = jax.random.split(jax.random.key(seed), 7)
    part_splits = jax.random.split(jax.random.fold_in(seeds[6], part), 7)
    queries = noise(part_splits[0], (TOKENS, HEADS * DH), 1.0, 6.0, ((0, 16),))
    latents = noise(part_splits[1], (N_CTX, LAT, LW), 1.0, 6.0, ((0, 8),))
    image_span = draw_image_span(jax.random.fold_in(jax.random.fold_in(seeds[6], part), 71), part)
    image_owner = draw_image_owner(jax.random.fold_in(jax.random.fold_in(seeds[6], part), 71), part)
    kv_weight = noise(seeds[4], (LW, 2, HEADS * DH), LW ** -0.5, 0.15625, ((0, 8), (2, 2)))
    attn_gate = jnp.clip(jax.random.uniform(seeds[5], (HEADS * DH,), jnp.float32, -1.5, 1.5) * block_scale(seeds[5], (HEADS * DH,), ((0, 2),), -0.4, 0.0), -1.5, 1.5)
    return dict(queries=queries, latents=latents, image_span=image_span, image_owner=image_owner, kv_weight=kv_weight, attn_gate=attn_gate)


def head_norm(x, size):
    shaped = x.reshape(x.shape[:-1] + (x.shape[-1] // size, size))
    mean = lax.optimization_barrier(jnp.mean(shaped, -1, keepdims=True))
    centered = shaped - mean
    spread = lax.optimization_barrier(jnp.mean(centered * centered, -1, keepdims=True))
    return (centered * lax.rsqrt(spread + 1e-05)).reshape(x.shape)

def reference(queries, latents, image_span, image_owner, kv_weight, attn_gate):
    width = HEADS * DH
    panels = latents[image_owner].reshape(IMAGES * LAT, LW)
    key_full = jnp.dot(panels, kv_weight[:, 0, :], preferred_element_type=jnp.float32)
    values = jnp.dot(panels, kv_weight[:, 1, :], preferred_element_type=jnp.float32).astype(jnp.bfloat16)
    keys = head_norm(key_full, DH).astype(jnp.bfloat16)
    keys = keys.reshape(IMAGES, LAT, HEADS, DH)
    values = values.reshape(IMAGES, LAT, HEADS, DH)
    query_norm = head_norm(queries.astype(jnp.float32), DH).astype(jnp.bfloat16)
    query_norm = query_norm.reshape(TOKENS, HEADS, DH)
    positions = jnp.arange(TOKENS, dtype=jnp.int32)
    inside = (positions[:, None] >= image_span[None, :, 0]) & (positions[:, None] < image_span[None, :, 1])
    has_image = jnp.any(inside, 1)
    which = lax.optimization_barrier(jnp.sum(jnp.where(inside, jnp.arange(IMAGES, dtype=jnp.int32)[None, :], 0), 1)).astype(jnp.int32)
    blocks = TOKENS // TOK_DEV

    def one_block(items):
        query_block, which_block, has_block = items
        key_block = keys[which_block].astype(jnp.float32)
        value_block = values[which_block].astype(jnp.float32)
        scores = jnp.einsum('bhd,blhd->bhl', query_block.astype(jnp.float32), key_block) * DH ** (-0.5)
        expo = jnp.exp(scores)
        probs = (expo / lax.optimization_barrier(jnp.sum(expo, -1, keepdims=True))).astype(jnp.bfloat16)
        attended = jnp.einsum('bhl,blhd->bhd', probs.astype(jnp.float32), value_block)
        return jnp.where(has_block[:, None, None], attended, jnp.float32(0.0))
    attended = lax.map(one_block, (query_norm.reshape(blocks, TOK_DEV, HEADS, DH), which.reshape(blocks, TOK_DEV), has_image.reshape(blocks, TOK_DEV)))
    attended = attended.reshape(TOKENS, width)
    return (jnp.tanh(attn_gate)[None, :] * attended).astype(jnp.bfloat16)
```

```python
import functools

import jax
import jax.numpy as jnp
from jax import lax
from jax.experimental import pallas as pl
from jax.experimental.pallas import tpu as pltpu
from jax.sharding import PartitionSpec as P

DH = 128
MAXIMG = 4


def head_norm(x, size):
    shaped = x.reshape(x.shape[:-1] + (x.shape[-1] // size, size))
    mean = jnp.mean(shaped, -1, keepdims=True)
    centered = shaped - mean
    spread = jnp.mean(centered * centered, -1, keepdims=True)
    return (centered * lax.rsqrt(spread + 1e-05)).reshape(x.shape)


def row_norm(x):
    centered = x - jnp.mean(x, -1, keepdims=True)
    spread = jnp.mean(centered * centered, -1, keepdims=True)
    return centered * lax.rsqrt(spread + 1e-05)


def attend_kernel(
    sizes, span_ref, owner_ref, gate_ref, got_ref, other_ref, out_ref, panel, weight
):
    ctx_count, rows, lat, tok, heads, images = sizes
    half = ctx_count // 2 * rows
    blocks = half // DH
    w_rows = heads * 2 * rows
    q_at = w_rows
    l_at = w_rows + heads * tok
    mine = lax.axis_index("head")
    for i in range(images):
        store = owner_ref[i]
        for b in range(blocks):
            at = slice(b * DH, (b + 1) * DH)
            panel[i * lat : (i + 1) * lat, at] = got_ref[store, l_at + b * lat : l_at + (b + 1) * lat, :]
            at = slice(half + b * DH, half + (b + 1) * DH)
            panel[i * lat : (i + 1) * lat, at] = other_ref[store, b * lat : (b + 1) * lat, :]
    for part in range(2):
        first = (mine if part == 0 else 1 - mine) * (ctx_count // 2)
        for s in range(ctx_count // 2):
            at = (part * (ctx_count // 2) + s) * rows
            for n in range(heads * 2):
                weight[at : at + rows, n * DH : (n + 1) * DH] = got_ref[
                    first + s, n * rows : (n + 1) * rows, :
                ]
    both = jnp.dot(panel[...], weight[...], preferred_element_type=jnp.float32)
    count = ctx_count * tok
    row = lax.broadcasted_iota(jnp.int32, (count, 1), 0)
    within = row % tok
    part = jnp.where(within < tok // 2, mine, 1 - mine)
    position = row // tok * tok + part * (tok // 2) + within % (tok // 2)
    slot = lax.broadcasted_iota(jnp.int32, (1, images * lat), 1) // lat
    low = jnp.zeros_like(slot)
    high = jnp.zeros_like(slot)
    for i in range(images):
        low = jnp.where(slot == i, span_ref[i, 0], low)
        high = jnp.where(slot == i, span_ref[i, 1], high)
    inside = (position >= low) & (position < high)
    for n in range(heads):
        keys = row_norm(both[:, n * 2 * DH : n * 2 * DH + DH]).astype(jnp.bfloat16)
        values = both[:, n * 2 * DH + DH : (n + 1) * 2 * DH].astype(jnp.bfloat16)
        query = got_ref[:, q_at + n * tok : q_at + (n + 1) * tok, :].reshape(count, DH)
        query = row_norm(query.astype(jnp.float32)).astype(jnp.bfloat16)
        scores = lax.dot_general(
            query, keys, (((1,), (1,)), ((), ())), preferred_element_type=jnp.float32
        ) * DH ** (-0.5)
        weighted = jnp.where(inside, jnp.exp(scores), 0.0)
        total = jnp.sum(weighted, -1, keepdims=True)
        total = jnp.where(total > 0.0, total, 1.0)
        probs = (weighted / total).astype(jnp.bfloat16)
        attended = jnp.dot(probs, values, preferred_element_type=jnp.float32)
        gate = jnp.tanh(gate_ref[n : n + 1, :])
        gated = (gate * attended).astype(jnp.bfloat16).reshape(ctx_count, 2, tok // 2, DH)
        for c in range(ctx_count):
            out_ref[c * 2 + mine, :, n * DH : (n + 1) * DH] = gated[c, 0]
            out_ref[c * 2 + 1 - mine, :, n * DH : (n + 1) * DH] = gated[c, 1]


def by_heads(queries, latents, image_span, image_owner, kv_weight, attn_gate):
    ctx_count = lax.axis_size("ctx")
    mine = lax.axis_index("head")
    place = lax.axis_index("ctx")
    tok = queries.shape[0] * 2
    width = kv_weight.shape[2]
    heads = width // DH // ctx_count
    rows = kv_weight.shape[0]
    lat, depth = latents.shape[1:]
    half = depth // 2
    images = image_span.shape[0]
    swap = [(0, 1), (1, 0)]
    kept = lax.dynamic_slice_in_dim(queries, mine * width, width, 1)
    sent = lax.dynamic_slice_in_dim(queries, (1 - mine) * width, width, 1)
    came = lax.ppermute(sent, "head", swap)
    query = jnp.concatenate([kept, came], 0).reshape(tok, ctx_count, heads, DH)
    query = query.transpose(1, 2, 0, 3).reshape(ctx_count, heads * tok, DH)
    weight = kv_weight.reshape(rows, 2, ctx_count, heads, DH).transpose(2, 3, 1, 0, 4)
    weight = weight.reshape(ctx_count, heads * 2 * rows, DH)
    share = lax.dynamic_slice_in_dim(latents[0], mine * half, half, 1)
    share = share.reshape(lat, half // DH, DH).transpose(1, 0, 2).reshape(1, lat * (half // DH), DH)
    share = jnp.broadcast_to(share, (ctx_count,) + share.shape[1:])
    outgoing = jnp.concatenate([weight, query, share], 1)
    got = lax.all_to_all(outgoing, "ctx", split_axis=0, concat_axis=0, tiled=True)
    other = lax.ppermute(got[:, heads * (2 * rows + tok) :, :], "head", swap)
    gate = lax.dynamic_slice_in_dim(attn_gate.reshape(-1, DH), place * heads, heads, 0)
    smem = pl.BlockSpec(memory_space=pltpu.SMEM)
    vmem = pl.BlockSpec(memory_space=pltpu.VMEM)
    gated = pl.pallas_call(
        functools.partial(attend_kernel, (ctx_count, rows, lat, tok, heads, images)),
        out_shape=jax.ShapeDtypeStruct((ctx_count * 2, tok // 2, heads * DH), jnp.bfloat16),
        in_specs=[smem, smem, vmem, vmem, vmem],
        out_specs=vmem,
        scratch_shapes=[
            pltpu.VMEM((images * lat, depth), jnp.bfloat16),
            pltpu.VMEM((depth, heads * 2 * DH), jnp.bfloat16),
        ],
        compiler_params=pltpu.CompilerParams(vmem_limit_bytes=40 * 1024 * 1024),
    )(image_span, image_owner, gate, got, other)
    back = lax.all_to_all(gated, ("ctx", "head"), split_axis=0, concat_axis=0, tiled=True)
    back = back.reshape(ctx_count, 2, tok // 2, heads * DH).transpose(2, 1, 0, 3)
    return back.reshape(tok // 2, 2 * width)


def by_tokens(queries, latents, image_span, image_owner, kv_weight, attn_gate):
    ctx_count = lax.axis_size("ctx")
    rows = lax.all_to_all(queries, "head", split_axis=1, concat_axis=0, tiled=True)
    tok = rows.shape[0]
    width = rows.shape[1]
    lat = latents.shape[1]
    images = image_span.shape[0]
    query_norm = head_norm(rows.astype(jnp.float32), DH).astype(jnp.bfloat16)
    starts = image_span[:, 0]
    ends = image_span[:, 1]
    block_low = jnp.arange(ctx_count, dtype=jnp.int32) * tok
    meets = (starts[None, :] < (block_low + tok)[:, None]) & (ends[None, :] > block_low[:, None])
    counts = jnp.sum(meets.astype(jnp.int32), 1)
    firsts = jnp.sum((ends[None, :] <= block_low[:, None]).astype(jnp.int32), 1)
    slot_iota = jnp.arange(MAXIMG, dtype=jnp.int32)
    wanted = jnp.minimum(firsts[:, None] + slot_iota[None, :], images - 1)
    live = slot_iota[None, :] < counts[:, None]
    holders = image_owner[wanted]
    pieces = lax.all_to_all(latents, "ctx", split_axis=2, concat_axis=0, tiled=True)
    outgoing = jnp.where(live[:, :, None, None], pieces[holders], jnp.zeros((), jnp.bfloat16))
    panels = lax.all_to_all(outgoing, "ctx", split_axis=0, concat_axis=3, tiled=True)
    gathered = lax.all_gather(kv_weight, "ctx", axis=0, tiled=True)
    flat_weight = gathered.reshape(gathered.shape[0], 2 * width)
    both = jnp.dot(
        panels.reshape(MAXIMG * lat, panels.shape[3]),
        flat_weight,
        preferred_element_type=jnp.float32,
    )
    keys_out = head_norm(both[:, :width], DH).astype(jnp.bfloat16)
    values_out = both[:, width:].astype(jnp.bfloat16)
    mine = lax.axis_index("ctx")
    positions = mine * tok + jnp.arange(tok, dtype=jnp.int32)
    inside = (positions[:, None] >= starts[None, :]) & (positions[:, None] < ends[None, :])
    has_image = jnp.any(inside, 1)
    which = jnp.sum(jnp.where(inside, jnp.arange(images, dtype=jnp.int32)[None, :], 0), 1)
    my_first = jnp.sum((ends <= mine * tok).astype(jnp.int32))
    slot = which - my_first
    heads_here = width // DH
    query_heads = query_norm.reshape(tok, heads_here, DH)
    key_heads = keys_out.reshape(MAXIMG * lat, heads_here, DH)
    value_heads = values_out.reshape(MAXIMG * lat, heads_here, DH)
    scores = jnp.einsum(
        "thd,khd->thk", query_heads, key_heads, preferred_element_type=jnp.float32
    ) * DH ** (-0.5)
    owner_slot = jnp.arange(MAXIMG * lat, dtype=jnp.int32) // lat
    selected = (has_image[:, None] & (owner_slot[None, :] == slot[:, None])).astype(jnp.float32)
    weighted = jnp.exp(scores) * selected[:, None, :]
    total = (
        jnp.sum(weighted, -1, keepdims=True) + (1.0 - has_image.astype(jnp.float32))[:, None, None]
    )
    probs = (weighted / total).astype(jnp.bfloat16)
    attended = jnp.einsum("thk,khd->thd", probs, value_heads, preferred_element_type=jnp.float32)
    attended = attended.reshape(tok, width)
    gated = (jnp.tanh(attn_gate)[None, :] * attended).astype(jnp.bfloat16)
    return lax.all_to_all(gated, "head", split_axis=0, concat_axis=1, tiled=True)


def shards(*args):
    ctx_count = lax.axis_size("ctx")
    weight = args[4]
    whole_heads = weight.shape[2] % (ctx_count * DH) == 0
    whole_blocks = args[1].shape[2] % (2 * DH) == 0 and weight.shape[0] % 16 == 0
    if whole_heads and whole_blocks and lax.axis_size("head") == 2 and ctx_count % 2 == 0:
        return by_heads(*args)
    return by_tokens(*args)


def solution(mesh):
    placed = (
        P(("groups", "ctx", "head"), None),
        P(("groups", "ctx"), None, None),
        P("groups", None),
        P("groups"),
        P("ctx", None, "head"),
        P("head"),
    )
    return jax.shard_map(
        shards,
        mesh=mesh,
        in_specs=placed,
        out_specs=P(("groups", "ctx", "head"), None),
        check_vma=False,
    )
```

```python
import functools

import jax
import jax.numpy as jnp
from jax import lax
from jax.experimental import pallas as pl
from jax.experimental.pallas import tpu as pltpu
from jax.sharding import PartitionSpec as P

DH = 128
MAXIMG = 4


def head_norm(x, size):
    shaped = x.reshape(x.shape[:-1] + (x.shape[-1] // size, size))
    mean = jnp.mean(shaped, -1, keepdims=True)
    centered = shaped - mean
    spread = jnp.mean(centered * centered, -1, keepdims=True)
    return (centered * lax.rsqrt(spread + 1e-05)).reshape(x.shape)


def row_norm(x):
    centered = x - jnp.mean(x, -1, keepdims=True)
    spread = jnp.mean(centered * centered, -1, keepdims=True)
    return centered * lax.rsqrt(spread + 1e-05)


def attend_kernel(sizes, mine_ref, theirs_ref, gate_ref, got_ref, *rest):
    stores, (out_ref, panel, weight) = rest[:-3], rest[-3:]
    ctx_count, rows, lat, part, heads, images = sizes
    half = ctx_count // 2 * rows
    blocks = half // DH
    q_at = heads * 2 * rows
    group = lax.axis_index("groups")
    place = lax.axis_index("ctx")
    core = lax.axis_index("head")
    for r, meta in enumerate((mine_ref, theirs_ref)):
        for i in range(images):
            turn = meta[i, 2] ^ place
            slot = turn // 2
            to = slice((r * images + i) * lat, (r * images + i + 1) * lat)
            for k in range(2):
                near, far = stores[4 * k + 2 * r : 4 * k + 2 * r + 2]
                for b in range(blocks):
                    come = slice(b * lat, (b + 1) * lat)
                    panel[to, k * half + b * DH : k * half + (b + 1) * DH] = jnp.where(
                        turn % 2 == 0, near[slot, come, :], far[slot, come, :]
                    )
    for k in range(2):
        first = (core ^ k) * (ctx_count // 2)
        for s in range(ctx_count // 2):
            to = slice(k * half + s * rows, k * half + (s + 1) * rows)
            for n in range(heads * 2):
                weight[to, n * DH : (n + 1) * DH] = got_ref[first + s, n * rows : (n + 1) * rows, :]
    both = jnp.dot(panel[...], weight[...], preferred_element_type=jnp.float32)
    count = ctx_count * 2 * part
    row = lax.broadcasted_iota(jnp.int32, (count, 1), 0)
    block = row // part
    position = (block // 2 * 2 + (block % 2 ^ core)) * part + row % part
    slot = lax.broadcasted_iota(jnp.int32, (1, images * lat), 1) // lat
    for r, meta in enumerate((mine_ref, theirs_ref)):
        low = jnp.zeros_like(slot)
        high = jnp.zeros_like(slot)
        for i in range(images):
            low = jnp.where(slot == i, meta[i, 0], low)
            high = jnp.where(slot == i, meta[i, 1], high)
        inside = (position >= low) & (position < high)
        these = both[r * images * lat : (r + 1) * images * lat, :]
        for n in range(heads):
            keys = row_norm(these[:, n * 2 * DH : n * 2 * DH + DH]).astype(jnp.bfloat16)
            values = these[:, n * 2 * DH + DH : (n + 1) * 2 * DH].astype(jnp.bfloat16)
            at = q_at + (n * 2 + r) * 2 * part
            query = got_ref[:, at : at + 2 * part, :].reshape(count, DH)
            query = row_norm(query.astype(jnp.float32)).astype(jnp.bfloat16)
            scores = lax.dot_general(
                query, keys, (((1,), (1,)), ((), ())), preferred_element_type=jnp.float32
            ) * DH ** (-0.5)
            weighted = jnp.where(inside, jnp.exp(scores), 0.0)
            total = jnp.sum(weighted, -1, keepdims=True)
            total = jnp.where(total > 0.0, total, 1.0)
            probs = (weighted / total).astype(jnp.bfloat16)
            attended = jnp.dot(probs, values, preferred_element_type=jnp.float32)
            gate = jnp.tanh(gate_ref[n : n + 1, :])
            gated = (gate * attended).astype(jnp.bfloat16).reshape(ctx_count, 2, part, DH)
            for c in range(ctx_count):
                for d in range(2):
                    to = ((group ^ r) * ctx_count + c) * 2 + (core ^ d)
                    out_ref[to, :, n * DH : (n + 1) * DH] = gated[c, d]


def split_kernel(query_ref, latents_ref, own_ref, core_ref, group_ref, both_ref, share_ref):
    group = lax.axis_index("groups")
    core = lax.axis_index("head")
    count, part = own_ref.shape[:2]
    for k, to in enumerate((own_ref, core_ref, group_ref, both_ref)):
        first = (core ^ k % 2) * 2 + (group ^ k // 2)
        for c in range(count):
            to[c] = query_ref[:, pl.ds(pl.multiple_of((first * count + c) * DH, DH), DH)]
    lat = latents_ref.shape[1]
    blocks = share_ref.shape[0] // lat
    for b in range(blocks):
        at = pl.ds(pl.multiple_of((core * blocks + b) * DH, DH), DH)
        share_ref[b * lat : (b + 1) * lat, :] = latents_ref[0, :, at]


def join_kernel(weight_ref, *rest):
    *pieces, out_ref = rest
    rows = weight_ref.shape[1]
    part = pieces[0].shape[1]
    out_ref[:, :rows, :] = weight_ref[...]
    for k, piece in enumerate(pieces):
        out_ref[:, rows + k * part : rows + (k + 1) * part, :] = piece[...]


def by_heads(queries, latents, image_span, image_owner, kv_weight, attn_gate):
    ctx_count = lax.axis_size("ctx")
    group = lax.axis_index("groups")
    place = lax.axis_index("ctx")
    core = lax.axis_index("head")
    part = queries.shape[0]
    width = kv_weight.shape[2]
    span = width // 2
    rows = kv_weight.shape[0]
    lat, depth = latents.shape[1:]
    images = image_span.shape[0]
    swap = [(0, 1), (1, 0)]
    smem = pl.BlockSpec(memory_space=pltpu.SMEM)
    vmem = pl.BlockSpec(memory_space=pltpu.VMEM)

    def across(x, turn):
        return lax.ppermute(x, "ctx", [(i, i ^ turn) for i in range(ctx_count)])

    piece = jax.ShapeDtypeStruct((ctx_count, part, DH), jnp.bfloat16)
    share = jax.ShapeDtypeStruct((depth // 2 // DH * lat, DH), jnp.bfloat16)
    *query, share = pl.pallas_call(
        split_kernel, out_shape=[piece] * 4 + [share], in_specs=[vmem] * 2, out_specs=[vmem] * 5
    )(queries, latents)
    query[1] = lax.ppermute(query[1], "head", swap)
    query[2] = lax.ppermute(query[2], "groups", swap)
    query[3] = lax.ppermute(query[3], ("groups", "head"), [(i, 3 - i) for i in range(4)])
    held = [share] + [across(share, 2 * k) for k in range(1, ctx_count // 2)]
    weight = lax.dynamic_slice_in_dim(kv_weight, group * span, span, 2)
    weight = weight.reshape(rows, 2, ctx_count, DH).transpose(2, 1, 0, 3)
    weight = weight.reshape(ctx_count, 2 * rows, DH)
    outgoing = pl.pallas_call(
        join_kernel,
        out_shape=jax.ShapeDtypeStruct((ctx_count, 2 * rows + 4 * part, DH), jnp.bfloat16),
        in_specs=[vmem] * 5,
        out_specs=vmem,
    )(weight, *query)
    outgoing, *held = lax.optimization_barrier((outgoing, *held))
    got = lax.all_to_all(outgoing, "ctx", split_axis=0, concat_axis=0, tiled=True)
    meta = jnp.concatenate([image_span, image_owner[:, None]], 1)
    meta_y = lax.ppermute(meta, "groups", swap)
    near = jnp.stack(held)
    near_y = lax.ppermute(near, "groups", swap)
    near_y, meta_y = lax.optimization_barrier((near_y, meta_y))
    stores = [near, across(near, 1), near_y, across(near_y, 1)]
    stores += [lax.ppermute(x, "head", swap) for x in stores]
    gate = lax.dynamic_slice_in_dim(attn_gate.reshape(-1, DH), group * ctx_count + place, 1, 0)
    gated = pl.pallas_call(
        functools.partial(attend_kernel, (ctx_count, rows, lat, part, 1, images)),
        out_shape=jax.ShapeDtypeStruct((ctx_count * 4, part, DH), jnp.bfloat16),
        in_specs=[smem] * 2 + [vmem] * 10,
        out_specs=vmem,
        scratch_shapes=[
            pltpu.VMEM((2 * images * lat, depth), jnp.bfloat16),
            pltpu.VMEM((depth, 2 * DH), jnp.bfloat16),
        ],
        compiler_params=pltpu.CompilerParams(vmem_limit_bytes=40 * 1024 * 1024),
    )(meta, meta_y, gate, got, *stores)
    every = ("groups", "ctx", "head")
    back = lax.all_to_all(gated, every, split_axis=0, concat_axis=0, tiled=True)
    back = back.reshape(2, ctx_count, 2, part, DH).transpose(3, 2, 0, 1, 4)
    return back.reshape(part, 2 * width)


def by_tokens(queries, latents, image_span, image_owner, kv_weight, attn_gate):
    ctx_count = lax.axis_size("ctx")
    rows = lax.all_to_all(queries, "head", split_axis=1, concat_axis=0, tiled=True)
    tok = rows.shape[0]
    width = rows.shape[1]
    lat = latents.shape[1]
    images = image_span.shape[0]
    query_norm = head_norm(rows.astype(jnp.float32), DH).astype(jnp.bfloat16)
    starts = image_span[:, 0]
    ends = image_span[:, 1]
    block_low = jnp.arange(ctx_count, dtype=jnp.int32) * tok
    meets = (starts[None, :] < (block_low + tok)[:, None]) & (ends[None, :] > block_low[:, None])
    counts = jnp.sum(meets.astype(jnp.int32), 1)
    firsts = jnp.sum((ends[None, :] <= block_low[:, None]).astype(jnp.int32), 1)
    slot_iota = jnp.arange(MAXIMG, dtype=jnp.int32)
    wanted = jnp.minimum(firsts[:, None] + slot_iota[None, :], images - 1)
    live = slot_iota[None, :] < counts[:, None]
    holders = image_owner[wanted]
    pieces = lax.all_to_all(latents, "ctx", split_axis=2, concat_axis=0, tiled=True)
    outgoing = jnp.where(live[:, :, None, None], pieces[holders], jnp.zeros((), jnp.bfloat16))
    panels = lax.all_to_all(outgoing, "ctx", split_axis=0, concat_axis=3, tiled=True)
    gathered = lax.all_gather(kv_weight, "ctx", axis=0, tiled=True)
    flat_weight = gathered.reshape(gathered.shape[0], 2 * width)
    both = jnp.dot(
        panels.reshape(MAXIMG * lat, panels.shape[3]),
        flat_weight,
        preferred_element_type=jnp.float32,
    )
    keys_out = head_norm(both[:, :width], DH).astype(jnp.bfloat16)
    values_out = both[:, width:].astype(jnp.bfloat16)
    mine = lax.axis_index("ctx")
    positions = mine * tok + jnp.arange(tok, dtype=jnp.int32)
    inside = (positions[:, None] >= starts[None, :]) & (positions[:, None] < ends[None, :])
    has_image = jnp.any(inside, 1)
    which = jnp.sum(jnp.where(inside, jnp.arange(images, dtype=jnp.int32)[None, :], 0), 1)
    my_first = jnp.sum((ends <= mine * tok).astype(jnp.int32))
    slot = which - my_first
    heads_here = width // DH
    query_heads = query_norm.reshape(tok, heads_here, DH)
    key_heads = keys_out.reshape(MAXIMG * lat, heads_here, DH)
    value_heads = values_out.reshape(MAXIMG * lat, heads_here, DH)
    scores = jnp.einsum(
        "thd,khd->thk", query_heads, key_heads, preferred_element_type=jnp.float32
    ) * DH ** (-0.5)
    owner_slot = jnp.arange(MAXIMG * lat, dtype=jnp.int32) // lat
    selected = (has_image[:, None] & (owner_slot[None, :] == slot[:, None])).astype(jnp.float32)
    weighted = jnp.exp(scores) * selected[:, None, :]
    total = (
        jnp.sum(weighted, -1, keepdims=True) + (1.0 - has_image.astype(jnp.float32))[:, None, None]
    )
    probs = (weighted / total).astype(jnp.bfloat16)
    attended = jnp.einsum("thk,khd->thd", probs, value_heads, preferred_element_type=jnp.float32)
    attended = attended.reshape(tok, width)
    gated = (jnp.tanh(attn_gate)[None, :] * attended).astype(jnp.bfloat16)
    return lax.all_to_all(gated, "head", split_axis=0, concat_axis=1, tiled=True)


def shards(*args):
    ctx_count = lax.axis_size("ctx")
    weight = args[4]
    pairs = lax.axis_size("groups") == 2 and lax.axis_size("head") == 2
    whole_heads = weight.shape[2] == 2 * ctx_count * DH
    whole_blocks = args[1].shape[2] % (2 * DH) == 0 and weight.shape[0] % 16 == 0
    if pairs and whole_heads and whole_blocks and ctx_count & (ctx_count - 1) == 0:
        return by_heads(*args)
    return by_tokens(*args)


def solution(mesh):
    placed = (
        P(("groups", "ctx", "head"), None),
        P(("groups", "ctx"), None, None),
        P("groups", None),
        P("groups"),
        P("ctx", None, "head"),
        P("head"),
    )
    return jax.shard_map(
        shards,
        mesh=mesh,
        in_specs=placed,
        out_specs=P(("groups", "ctx", "head"), None),
        check_vma=False,
    )
```

```python
import functools

import jax
import jax.numpy as jnp
from jax import lax
from jax.experimental import pallas as pl
from jax.experimental.pallas import tpu as pltpu
from jax.sharding import PartitionSpec as P

DH = 128
MAXIMG = 4


def head_norm(x, size):
    shaped = x.reshape(x.shape[:-1] + (x.shape[-1] // size, size))
    mean = jnp.mean(shaped, -1, keepdims=True)
    centered = shaped - mean
    spread = jnp.mean(centered * centered, -1, keepdims=True)
    return (centered * lax.rsqrt(spread + 1e-05)).reshape(x.shape)


def row_norm(x):
    centered = x - jnp.mean(x, -1, keepdims=True)
    spread = jnp.mean(centered * centered, -1, keepdims=True)
    return centered * lax.rsqrt(spread + 1e-05)


def panel_kernel(meta_ref, meta_y_ref, *rest):
    *stores, panel_ref = rest
    images = meta_ref.shape[1]
    lat, half = stores[0].shape[1:]
    place = lax.axis_index("ctx")
    for r, meta in enumerate((meta_ref, meta_y_ref)):
        for i in range(images):
            turn = meta[2, i] ^ place
            slot = turn // 2
            to = slice((r * images + i) * lat, (r * images + i + 1) * lat)
            for k in range(2):
                near, far = stores[4 * k + 2 * r : 4 * k + 2 * r + 2]
                panel_ref[to, k * half : (k + 1) * half] = jnp.where(turn % 2 == 0, near[slot], far[slot])


def attend_kernel(sizes, meta_ref, meta_y_ref, gate_ref, got_ref, panel, out_ref, weight):
    ctx_count, rows, lat, part, heads, images = sizes
    half = ctx_count // 2 * rows
    piece = rows // 2
    group = lax.axis_index("groups")
    core = lax.axis_index("head")
    for k in range(2):
        first = (core ^ k) * (ctx_count // 2)
        for s in range(ctx_count // 2):
            for g in range(2):
                to = slice(k * half + s * rows + g * piece, k * half + s * rows + (g + 1) * piece)
                for n in range(heads * 2):
                    weight[to, n * DH : (n + 1) * DH] = got_ref[
                        g * ctx_count + first + s, n * piece : (n + 1) * piece, :
                    ]
    count = ctx_count * 2 * part
    queries = []
    for r in range(2):
        query = got_ref[pl.ds((group ^ r) * ctx_count, ctx_count), rows : rows + 2 * part, :]
        queries.append(row_norm(query.reshape(count, DH).astype(jnp.float32)).astype(jnp.bfloat16))
    gate = jnp.tanh(gate_ref[...])
    row = lax.broadcasted_iota(jnp.int32, (1, count), 1)
    block = row // part
    position = (block // 2 * 2 + (block % 2 ^ core)) * part + row % part
    both = jnp.dot(panel[...], weight[...], preferred_element_type=jnp.float32)
    keys = row_norm(both[:, :DH]).astype(jnp.bfloat16)
    values = both[:, DH:].astype(jnp.bfloat16)
    for r, spans in enumerate((meta_ref, meta_y_ref)):
        at = r * images * lat
        scores = lax.dot_general(
            keys[at : at + images * lat], queries[r], (((1,), (1,)), ((), ())), preferred_element_type=jnp.float32
        ) * DH ** (-0.5)
        weighted = []
        for i in range(images):
            inside = (position >= spans[0, i]) & (position < spans[1, i])
            weighted.append(jnp.where(inside, jnp.exp(scores[i * lat : (i + 1) * lat]), 0.0))
        total = sum(jnp.sum(w, 0, keepdims=True) for w in weighted)
        scale = 1.0 / jnp.where(total > 0.0, total, 1.0)
        probs = jnp.concatenate([(w * scale).astype(jnp.bfloat16) for w in weighted], 0)
        attended = lax.dot_general(values[at : at + images * lat], probs, (((0,), (0,)), ((), ())), preferred_element_type=jnp.float32).T
        gated = (gate * attended).astype(jnp.bfloat16).reshape(ctx_count, 2, part, DH)
        for c in range(ctx_count):
            for d in range(2):
                to = ((group ^ r) * ctx_count + c) * 2 + (core ^ d)
                out_ref[to] = gated[c, d]


def split_kernel(query_ref, own_ref, core_ref):
    core = lax.axis_index("head")
    count = own_ref.shape[0]
    for k, to in enumerate((own_ref, core_ref)):
        for c in range(count):
            to[c] = query_ref[:, pl.ds(pl.multiple_of(((core ^ k) * count + c) * DH, DH), DH)]


def join_kernel(weight_ref, *rest):
    *pieces, out_ref = rest
    rows = weight_ref.shape[1]
    part = pieces[0].shape[1]
    out_ref[:, :rows, :] = weight_ref[...]
    for k, piece in enumerate(pieces):
        out_ref[:, rows + k * part : rows + (k + 1) * part, :] = piece[...]


def by_heads(queries, latents, image_span, image_owner, kv_weight, attn_gate):
    ctx_count = lax.axis_size("ctx")
    group = lax.axis_index("groups")
    place = lax.axis_index("ctx")
    core = lax.axis_index("head")
    part = queries.shape[0]
    width = kv_weight.shape[2]
    span = width // 2
    rows = kv_weight.shape[0]
    lat, depth = latents.shape[1:]
    images = image_span.shape[0]
    swap = [(0, 1), (1, 0)]
    smem = pl.BlockSpec(memory_space=pltpu.SMEM)
    vmem = pl.BlockSpec(memory_space=pltpu.VMEM)

    def across(x, turn):
        return lax.ppermute(x, "ctx", [(i, i ^ turn) for i in range(ctx_count)])

    share = lax.dynamic_slice_in_dim(latents[0], core * (depth // 2), depth // 2, 1)
    held = [share] + [across(share, 2 * k) for k in range(1, ctx_count // 2)]
    piece = jax.ShapeDtypeStruct((2 * ctx_count, part, DH), jnp.bfloat16)
    own, sent = pl.pallas_call(
        split_kernel,
        out_shape=[piece] * 2,
        in_specs=[vmem],
        out_specs=[vmem] * 2,
        compiler_params=pltpu.CompilerParams(vmem_limit_bytes=4 * 1024 * 1024),
    )(queries)
    came = lax.ppermute(sent, "head", swap)
    own, meta = lax.optimization_barrier((own, (image_span.T, image_owner[None, :])))
    meta = jnp.concatenate(meta, 0)
    meta_y = lax.ppermute(meta, "groups", swap)
    half = rows // 2
    weight = lax.dynamic_slice_in_dim(kv_weight, group * half, half, 0)
    weight = weight.reshape(half, 2, 2 * ctx_count, DH).transpose(2, 1, 0, 3)
    weight = weight.reshape(2 * ctx_count, 2 * half, DH)
    outgoing = pl.pallas_call(
        join_kernel,
        out_shape=jax.ShapeDtypeStruct((2 * ctx_count, 2 * half + 2 * part, DH), jnp.bfloat16),
        in_specs=[vmem] * 3,
        out_specs=vmem,
        compiler_params=pltpu.CompilerParams(vmem_limit_bytes=6 * 1024 * 1024),
    )(weight, own, came)
    outgoing, meta_y, *held = lax.optimization_barrier((outgoing, meta_y, *held))
    got = lax.all_to_all(outgoing, ("groups", "ctx"), split_axis=0, concat_axis=0, tiled=True)
    near = jnp.stack(held)
    near_y, far = lax.optimization_barrier((lax.ppermute(near, "groups", swap), across(near, 1)))
    stores = [near, far, near_y, across(near_y, 1)]
    stores += [lax.ppermute(x, "head", swap) for x in stores]
    gate = lax.dynamic_slice_in_dim(attn_gate.reshape(-1, DH), group * ctx_count + place, 1, 0)
    panel = pl.pallas_call(
        panel_kernel,
        out_shape=jax.ShapeDtypeStruct((2 * images * lat, depth), jnp.bfloat16),
        in_specs=[smem] * 2 + [vmem] * 8,
        out_specs=vmem,
        cost_estimate=pl.CostEstimate(flops=9_200_000_000, bytes_accessed=4 * 1024 * 1024, transcendentals=0),
        compiler_params=pltpu.CompilerParams(vmem_limit_bytes=8 * 1024 * 1024),
    )(meta, meta_y, *stores)
    gated = pl.pallas_call(
        functools.partial(attend_kernel, (ctx_count, rows, lat, part, 1, images)),
        out_shape=jax.ShapeDtypeStruct((ctx_count * 4, part, DH), jnp.bfloat16),
        in_specs=[smem] * 2 + [vmem] * 3,
        out_specs=vmem,
        scratch_shapes=[pltpu.VMEM((depth, 2 * DH), jnp.bfloat16)],
        compiler_params=pltpu.CompilerParams(vmem_limit_bytes=16 * 1024 * 1024),
    )(meta, meta_y, gate, got, panel)
    every = ("groups", "ctx", "head")
    back = lax.all_to_all(gated, every, split_axis=0, concat_axis=0, tiled=True)
    back = back.reshape(2, ctx_count, 2, part, DH).transpose(3, 2, 0, 1, 4)
    return back.reshape(part, 2 * width)


def by_tokens(queries, latents, image_span, image_owner, kv_weight, attn_gate):
    ctx_count = lax.axis_size("ctx")
    rows = lax.all_to_all(queries, "head", split_axis=1, concat_axis=0, tiled=True)
    tok = rows.shape[0]
    width = rows.shape[1]
    lat = latents.shape[1]
    images = image_span.shape[0]
    query_norm = head_norm(rows.astype(jnp.float32), DH).astype(jnp.bfloat16)
    starts = image_span[:, 0]
    ends = image_span[:, 1]
    block_low = jnp.arange(ctx_count, dtype=jnp.int32) * tok
    meets = (starts[None, :] < (block_low + tok)[:, None]) & (ends[None, :] > block_low[:, None])
    counts = jnp.sum(meets.astype(jnp.int32), 1)
    firsts = jnp.sum((ends[None, :] <= block_low[:, None]).astype(jnp.int32), 1)
    slot_iota = jnp.arange(MAXIMG, dtype=jnp.int32)
    wanted = jnp.minimum(firsts[:, None] + slot_iota[None, :], images - 1)
    live = slot_iota[None, :] < counts[:, None]
    holders = image_owner[wanted]
    pieces = lax.all_to_all(latents, "ctx", split_axis=2, concat_axis=0, tiled=True)
    outgoing = jnp.where(live[:, :, None, None], pieces[holders], jnp.zeros((), jnp.bfloat16))
    panels = lax.all_to_all(outgoing, "ctx", split_axis=0, concat_axis=3, tiled=True)
    gathered = lax.all_gather(kv_weight, "ctx", axis=0, tiled=True)
    flat_weight = gathered.reshape(gathered.shape[0], 2 * width)
    both = jnp.dot(
        panels.reshape(MAXIMG * lat, panels.shape[3]),
        flat_weight,
        preferred_element_type=jnp.float32,
    )
    keys_out = head_norm(both[:, :width], DH).astype(jnp.bfloat16)
    values_out = both[:, width:].astype(jnp.bfloat16)
    mine = lax.axis_index("ctx")
    positions = mine * tok + jnp.arange(tok, dtype=jnp.int32)
    inside = (positions[:, None] >= starts[None, :]) & (positions[:, None] < ends[None, :])
    has_image = jnp.any(inside, 1)
    which = jnp.sum(jnp.where(inside, jnp.arange(images, dtype=jnp.int32)[None, :], 0), 1)
    my_first = jnp.sum((ends <= mine * tok).astype(jnp.int32))
    slot = which - my_first
    heads_here = width // DH
    query_heads = query_norm.reshape(tok, heads_here, DH)
    key_heads = keys_out.reshape(MAXIMG * lat, heads_here, DH)
    value_heads = values_out.reshape(MAXIMG * lat, heads_here, DH)
    scores = jnp.einsum(
        "thd,khd->thk", query_heads, key_heads, preferred_element_type=jnp.float32
    ) * DH ** (-0.5)
    owner_slot = jnp.arange(MAXIMG * lat, dtype=jnp.int32) // lat
    selected = (has_image[:, None] & (owner_slot[None, :] == slot[:, None])).astype(jnp.float32)
    weighted = jnp.exp(scores) * selected[:, None, :]
    total = (
        jnp.sum(weighted, -1, keepdims=True) + (1.0 - has_image.astype(jnp.float32))[:, None, None]
    )
    probs = (weighted / total).astype(jnp.bfloat16)
    attended = jnp.einsum("thk,khd->thd", probs, value_heads, preferred_element_type=jnp.float32)
    attended = attended.reshape(tok, width)
    gated = (jnp.tanh(attn_gate)[None, :] * attended).astype(jnp.bfloat16)
    return lax.all_to_all(gated, "head", split_axis=0, concat_axis=1, tiled=True)


def shards(*args):
    ctx_count = lax.axis_size("ctx")
    weight = args[4]
    pairs = lax.axis_size("groups") == 2 and lax.axis_size("head") == 2
    whole_heads = weight.shape[2] == 2 * ctx_count * DH
    whole_blocks = args[1].shape[2] % (2 * DH) == 0 and weight.shape[0] % 32 == 0
    if pairs and whole_heads and whole_blocks and ctx_count & (ctx_count - 1) == 0:
        return by_heads(*args)
    return by_tokens(*args)


def solution(mesh):
    placed = (
        P(("groups", "ctx", "head"), None),
        P(("groups", "ctx"), None, None),
        P("groups", None),
        P("groups"),
        P("ctx", None, "head"),
        P("head"),
    )
    return jax.shard_map(
        shards,
        mesh=mesh,
        in_specs=placed,
        out_specs=P(("groups", "ctx", "head"), None),
        check_vma=False,
    )
```

```python
import functools

import jax
import jax.numpy as jnp
from jax import lax
from jax.experimental import pallas as pl
from jax.experimental.pallas import tpu as pltpu
from jax.sharding import PartitionSpec as P

DH = 128
MAXIMG = 4


def head_norm(x, size):
    shaped = x.reshape(x.shape[:-1] + (x.shape[-1] // size, size))
    mean = jnp.mean(shaped, -1, keepdims=True)
    centered = shaped - mean
    spread = jnp.mean(centered * centered, -1, keepdims=True)
    return (centered * lax.rsqrt(spread + 1e-05)).reshape(x.shape)


def row_norm(x):
    centered = x - jnp.mean(x, -1, keepdims=True)
    spread = jnp.mean(centered * centered, -1, keepdims=True)
    return centered * lax.rsqrt(spread + 1e-05)


def panel_kernel(meta_ref, meta_y_ref, *rest):
    *stores, panel_ref = rest
    images = meta_ref.shape[1]
    lat, half = stores[0].shape[1:]
    place = lax.axis_index("ctx")
    for r, meta in enumerate((meta_ref, meta_y_ref)):
        for i in range(images):
            turn = meta[2, i] ^ place
            slot = turn // 2
            to = slice((r * images + i) * lat, (r * images + i + 1) * lat)
            for k in range(2):
                near, far = stores[4 * k + 2 * r : 4 * k + 2 * r + 2]
                panel_ref[to, k * half : (k + 1) * half] = jnp.where(turn % 2 == 0, near[slot], far[slot])


def attend_kernel(sizes, meta_ref, meta_y_ref, gate_ref, got_ref, panel, out_ref, weight):
    ctx_count, rows, lat, part, images = sizes
    half = ctx_count // 2 * rows
    piece = rows // 2
    size = images * lat
    count = ctx_count * 2 * part
    group = lax.axis_index("groups")
    core = lax.axis_index("head")
    metas = (meta_ref, meta_y_ref)
    for k in range(2):
        first = (core ^ k) * (ctx_count // 2)
        for s in range(ctx_count // 2):
            for g in range(2):
                at = k * half + s * rows + g * piece
                for n in range(2):
                    weight[at : at + piece, n * DH : (n + 1) * DH] = got_ref[
                        g * ctx_count + first + s, n * piece : (n + 1) * piece, :
                    ]
    queries = []
    for r in range(2):
        query = got_ref[pl.ds((group ^ r) * ctx_count, ctx_count), rows : rows + 2 * part, :]
        queries.append(row_norm(query.reshape(count, DH).astype(jnp.float32)).astype(jnp.bfloat16))
    gate = jnp.tanh(gate_ref[...])
    row = lax.broadcasted_iota(jnp.int32, (1, count), 1)
    block = row // part
    position = (block // 2 * 2 + (block % 2 ^ core)) * part + row % part

    def project(r):
        both = jnp.dot(
            panel[r * size : (r + 1) * size, :], weight[...], preferred_element_type=jnp.float32
        )
        return row_norm(both[:, :DH]).astype(jnp.bfloat16), both[:, DH:].astype(jnp.bfloat16)

    def score(r, keys):
        return lax.dot_general(
            keys, queries[r], (((1,), (1,)), ((), ())), preferred_element_type=jnp.float32
        ) * DH ** (-0.5)

    def finish(r, scores, values):
        weighted = []
        for i in range(images):
            inside = (position >= metas[r][0, i]) & (position < metas[r][1, i])
            weighted.append(jnp.where(inside, jnp.exp(scores[i * lat : (i + 1) * lat]), 0.0))
        total = sum(jnp.sum(w, 0, keepdims=True) for w in weighted)
        scale = 1.0 / jnp.where(total > 0.0, total, 1.0)
        probs = jnp.concatenate([(w * scale).astype(jnp.bfloat16) for w in weighted], 0)
        attended = lax.dot_general(
            values, probs, (((0,), (0,)), ((), ())), preferred_element_type=jnp.float32
        ).T
        gated = (gate * attended).astype(jnp.bfloat16).reshape(ctx_count, 2, part, DH)
        for c in range(ctx_count):
            for d in range(2):
                out_ref[((group ^ r) * ctx_count + c) * 2 + (core ^ d)] = gated[c, d]

    projected = [project(r) for r in range(2)]
    scores = [score(r, projected[r][0]) for r in range(2)]
    for r in range(2):
        finish(r, scores[r], projected[r][1])


def split_kernel(query_ref, own_ref, core_ref):
    core = lax.axis_index("head")
    count = own_ref.shape[0]
    for k, to in enumerate((own_ref, core_ref)):
        for c in range(count):
            to[c] = query_ref[:, pl.ds(pl.multiple_of(((core ^ k) * count + c) * DH, DH), DH)]


def join_kernel(weight_ref, *rest):
    *pieces, out_ref = rest
    rows = weight_ref.shape[1]
    part = pieces[0].shape[1]
    out_ref[:, :rows, :] = weight_ref[...]
    for k, piece in enumerate(pieces):
        out_ref[:, rows + k * part : rows + (k + 1) * part, :] = piece[...]


def merge_kernel(back_ref, out_ref):
    count = back_ref.shape[0] // 4
    for n in range(4 * count):
        g, c, h = n // (2 * count), n // 2 % count, n % 2
        at = ((h * 2 + g) * count + c) * DH
        out_ref[:, at : at + DH] = back_ref[n]


def by_heads(queries, latents, image_span, image_owner, kv_weight, attn_gate):
    ctx_count = lax.axis_size("ctx")
    group = lax.axis_index("groups")
    place = lax.axis_index("ctx")
    core = lax.axis_index("head")
    part = queries.shape[0]
    width = kv_weight.shape[2]
    span = width // 2
    rows = kv_weight.shape[0]
    lat, depth = latents.shape[1:]
    images = image_span.shape[0]
    swap = [(0, 1), (1, 0)]
    smem = pl.BlockSpec(memory_space=pltpu.SMEM)
    vmem = pl.BlockSpec(memory_space=pltpu.VMEM)

    def across(x, turn):
        return lax.ppermute(x, "ctx", [(i, i ^ turn) for i in range(ctx_count)])

    share = lax.dynamic_slice_in_dim(latents[0], core * (depth // 2), depth // 2, 1)
    held = [share] + [across(share, 2 * k) for k in range(1, ctx_count // 2)]
    piece = jax.ShapeDtypeStruct((2 * ctx_count, part, DH), jnp.bfloat16)
    own, sent = pl.pallas_call(
        split_kernel,
        out_shape=[piece] * 2,
        in_specs=[vmem],
        out_specs=[vmem] * 2,
        compiler_params=pltpu.CompilerParams(vmem_limit_bytes=4 * 1024 * 1024),
    )(queries)
    came = lax.ppermute(sent, "head", swap)
    own, meta = lax.optimization_barrier((own, (image_span.T, image_owner[None, :])))
    meta = jnp.concatenate(meta, 0)
    meta_y = lax.ppermute(meta, "groups", swap)
    half = rows // 2
    weight = lax.dynamic_slice_in_dim(kv_weight, group * half, half, 0)
    weight = weight.reshape(half, 2, 2 * ctx_count, DH).transpose(2, 1, 0, 3)
    weight = weight.reshape(2 * ctx_count, 2 * half, DH)
    outgoing = pl.pallas_call(
        join_kernel,
        out_shape=jax.ShapeDtypeStruct((2 * ctx_count, 2 * half + 2 * part, DH), jnp.bfloat16),
        in_specs=[vmem] * 3,
        out_specs=vmem,
        compiler_params=pltpu.CompilerParams(vmem_limit_bytes=6 * 1024 * 1024),
    )(weight, own, came)
    outgoing, meta_y, *held = lax.optimization_barrier((outgoing, meta_y, *held))
    got = lax.all_to_all(outgoing, ("groups", "ctx"), split_axis=0, concat_axis=0, tiled=True)
    near = jnp.stack(held)
    near_y, far = lax.optimization_barrier((lax.ppermute(near, "groups", swap), across(near, 1)))
    stores = [near, far, near_y, across(near_y, 1)]
    stores += [lax.ppermute(x, "head", swap) for x in stores]
    gate = lax.dynamic_slice_in_dim(attn_gate.reshape(-1, DH), group * ctx_count + place, 1, 0)
    panel = pl.pallas_call(
        panel_kernel,
        out_shape=jax.ShapeDtypeStruct((2 * images * lat, depth), jnp.bfloat16),
        in_specs=[smem] * 2 + [vmem] * 8,
        out_specs=vmem,
        cost_estimate=pl.CostEstimate(flops=9_200_000_000, bytes_accessed=4 * 1024 * 1024, transcendentals=0),
        compiler_params=pltpu.CompilerParams(vmem_limit_bytes=8 * 1024 * 1024),
    )(meta, meta_y, *stores)
    gated = pl.pallas_call(
        functools.partial(attend_kernel, (ctx_count, rows, lat, part, images)),
        out_shape=jax.ShapeDtypeStruct((ctx_count * 4, part, DH), jnp.bfloat16),
        in_specs=[smem] * 2 + [vmem] * 3,
        out_specs=vmem,
        scratch_shapes=[pltpu.VMEM((depth, 2 * DH), jnp.bfloat16)],
        compiler_params=pltpu.CompilerParams(vmem_limit_bytes=16 * 1024 * 1024),
    )(meta, meta_y, gate, got, panel)
    every = ("groups", "ctx", "head")
    back = lax.all_to_all(gated, every, split_axis=0, concat_axis=0, tiled=True)
    return pl.pallas_call(
        merge_kernel,
        out_shape=jax.ShapeDtypeStruct((part, 2 * width), jnp.bfloat16),
        in_specs=[vmem],
        out_specs=vmem,
        compiler_params=pltpu.CompilerParams(vmem_limit_bytes=4 * 1024 * 1024),
    )(back)


def by_tokens(queries, latents, image_span, image_owner, kv_weight, attn_gate):
    ctx_count = lax.axis_size("ctx")
    rows = lax.all_to_all(queries, "head", split_axis=1, concat_axis=0, tiled=True)
    tok = rows.shape[0]
    width = rows.shape[1]
    lat = latents.shape[1]
    images = image_span.shape[0]
    query_norm = head_norm(rows.astype(jnp.float32), DH).astype(jnp.bfloat16)
    starts = image_span[:, 0]
    ends = image_span[:, 1]
    block_low = jnp.arange(ctx_count, dtype=jnp.int32) * tok
    meets = (starts[None, :] < (block_low + tok)[:, None]) & (ends[None, :] > block_low[:, None])
    counts = jnp.sum(meets.astype(jnp.int32), 1)
    firsts = jnp.sum((ends[None, :] <= block_low[:, None]).astype(jnp.int32), 1)
    slot_iota = jnp.arange(MAXIMG, dtype=jnp.int32)
    wanted = jnp.minimum(firsts[:, None] + slot_iota[None, :], images - 1)
    live = slot_iota[None, :] < counts[:, None]
    holders = image_owner[wanted]
    pieces = lax.all_to_all(latents, "ctx", split_axis=2, concat_axis=0, tiled=True)
    outgoing = jnp.where(live[:, :, None, None], pieces[holders], jnp.zeros((), jnp.bfloat16))
    panels = lax.all_to_all(outgoing, "ctx", split_axis=0, concat_axis=3, tiled=True)
    gathered = lax.all_gather(kv_weight, "ctx", axis=0, tiled=True)
    flat_weight = gathered.reshape(gathered.shape[0], 2 * width)
    both = jnp.dot(
        panels.reshape(MAXIMG * lat, panels.shape[3]),
        flat_weight,
        preferred_element_type=jnp.float32,
    )
    keys_out = head_norm(both[:, :width], DH).astype(jnp.bfloat16)
    values_out = both[:, width:].astype(jnp.bfloat16)
    mine = lax.axis_index("ctx")
    positions = mine * tok + jnp.arange(tok, dtype=jnp.int32)
    inside = (positions[:, None] >= starts[None, :]) & (positions[:, None] < ends[None, :])
    has_image = jnp.any(inside, 1)
    which = jnp.sum(jnp.where(inside, jnp.arange(images, dtype=jnp.int32)[None, :], 0), 1)
    my_first = jnp.sum((ends <= mine * tok).astype(jnp.int32))
    slot = which - my_first
    heads_here = width // DH
    query_heads = query_norm.reshape(tok, heads_here, DH)
    key_heads = keys_out.reshape(MAXIMG * lat, heads_here, DH)
    value_heads = values_out.reshape(MAXIMG * lat, heads_here, DH)
    scores = jnp.einsum(
        "thd,khd->thk", query_heads, key_heads, preferred_element_type=jnp.float32
    ) * DH ** (-0.5)
    owner_slot = jnp.arange(MAXIMG * lat, dtype=jnp.int32) // lat
    selected = (has_image[:, None] & (owner_slot[None, :] == slot[:, None])).astype(jnp.float32)
    weighted = jnp.exp(scores) * selected[:, None, :]
    total = (
        jnp.sum(weighted, -1, keepdims=True) + (1.0 - has_image.astype(jnp.float32))[:, None, None]
    )
    probs = (weighted / total).astype(jnp.bfloat16)
    attended = jnp.einsum("thk,khd->thd", probs, value_heads, preferred_element_type=jnp.float32)
    attended = attended.reshape(tok, width)
    gated = (jnp.tanh(attn_gate)[None, :] * attended).astype(jnp.bfloat16)
    return lax.all_to_all(gated, "head", split_axis=0, concat_axis=1, tiled=True)


def shards(*args):
    ctx_count = lax.axis_size("ctx")
    weight = args[4]
    pairs = lax.axis_size("groups") == 2 and lax.axis_size("head") == 2
    whole_heads = weight.shape[2] == 2 * ctx_count * DH
    whole_blocks = args[1].shape[2] % (2 * DH) == 0 and weight.shape[0] % 32 == 0
    if pairs and whole_heads and whole_blocks and ctx_count & (ctx_count - 1) == 0:
        return by_heads(*args)
    return by_tokens(*args)


def solution(mesh):
    placed = (
        P(("groups", "ctx", "head"), None),
        P(("groups", "ctx"), None, None),
        P("groups", None),
        P("groups"),
        P("ctx", None, "head"),
        P("head"),
    )
    return jax.shard_map(
        shards,
        mesh=mesh,
        in_specs=placed,
        out_specs=P(("groups", "ctx", "head"), None),
        check_vma=False,
    )
```

```python
import functools

import jax
import jax.numpy as jnp
from jax import lax
from jax.experimental import pallas as pl
from jax.experimental.pallas import tpu as pltpu
from jax.sharding import PartitionSpec as P

DH = 128
MAXIMG = 4


def head_norm(x, size):
    shaped = x.reshape(x.shape[:-1] + (x.shape[-1] // size, size))
    mean = jnp.mean(shaped, -1, keepdims=True)
    centered = shaped - mean
    spread = jnp.mean(centered * centered, -1, keepdims=True)
    return (centered * lax.rsqrt(spread + 1e-05)).reshape(x.shape)


def row_norm(x):
    centered = x - jnp.mean(x, -1, keepdims=True)
    spread = jnp.mean(centered * centered, -1, keepdims=True)
    return centered * lax.rsqrt(spread + 1e-05)


def panel_kernel(meta_ref, meta_y_ref, *rest):
    *stores, panel_ref = rest
    images = meta_ref.shape[1]
    lat, half = stores[0].shape[1:]
    place = lax.axis_index("ctx")
    for r, meta in enumerate((meta_ref, meta_y_ref)):
        for i in range(images):
            turn = meta[2, i] ^ place
            slot = turn // 2
            to = slice((r * images + i) * lat, (r * images + i + 1) * lat)
            for k in range(2):
                near, far, near_y, far_y, last_y = stores[5 * k : 5 * k + 5]
                cut = far_y.shape[0]
                if r == 0:
                    one, other = near[slot], far[slot]
                else:
                    one, other = near_y[slot], jnp.where(slot < cut, far_y[slot % cut], last_y[slot % cut])
                panel_ref[to, k * half : (k + 1) * half] = jnp.where(turn % 2 == 0, one, other)


def attend_kernel(sizes, meta_ref, meta_y_ref, gate_ref, got_ref, panel, out_ref, weight):
    ctx_count, rows, lat, part, images = sizes
    half = ctx_count // 2 * rows
    piece = rows // 2
    size = images * lat
    count = ctx_count * 2 * part
    group = lax.axis_index("groups")
    core = lax.axis_index("head")
    metas = (meta_ref, meta_y_ref)
    for k in range(2):
        first = (core ^ k) * (ctx_count // 2)
        for s in range(ctx_count // 2):
            for g in range(2):
                at = k * half + s * rows + g * piece
                for n in range(2):
                    weight[at : at + piece, n * DH : (n + 1) * DH] = got_ref[
                        g * ctx_count + first + s, n * piece : (n + 1) * piece, :
                    ]
    queries = []
    for r in range(2):
        query = got_ref[pl.ds((group ^ r) * ctx_count, ctx_count), rows : rows + 2 * part, :]
        queries.append(row_norm(query.reshape(count, DH).astype(jnp.float32)).astype(jnp.bfloat16))
    gate = jnp.tanh(gate_ref[...])
    row = lax.broadcasted_iota(jnp.int32, (1, count), 1)
    block = row // part
    position = (block // 2 * 2 + (block % 2 ^ core)) * part + row % part

    def project(r):
        both = jnp.dot(
            panel[r * size : (r + 1) * size, :], weight[...], preferred_element_type=jnp.float32
        )
        return row_norm(both[:, :DH]).astype(jnp.bfloat16), both[:, DH:].astype(jnp.bfloat16)

    def score(r, keys):
        return lax.dot_general(
            keys, queries[r], (((1,), (1,)), ((), ())), preferred_element_type=jnp.float32
        ) * DH ** (-0.5)

    def finish(r, scores, values):
        weighted = []
        for i in range(images):
            inside = (position >= metas[r][0, i]) & (position < metas[r][1, i])
            weighted.append(jnp.where(inside, jnp.exp(scores[i * lat : (i + 1) * lat]), 0.0))
        total = sum(jnp.sum(w, 0, keepdims=True) for w in weighted)
        scale = 1.0 / jnp.where(total > 0.0, total, 1.0)
        probs = jnp.concatenate([(w * scale).astype(jnp.bfloat16) for w in weighted], 0)
        attended = lax.dot_general(
            values, probs, (((0,), (0,)), ((), ())), preferred_element_type=jnp.float32
        ).T
        gated = (gate * attended).astype(jnp.bfloat16).reshape(ctx_count, 2, part, DH)
        for c in range(ctx_count):
            for d in range(2):
                out_ref[((group ^ r) * ctx_count + c) * 2 + (core ^ d)] = gated[c, d]

    projected = [project(r) for r in range(2)]
    scores = [score(r, projected[r][0]) for r in range(2)]
    for r in range(2):
        finish(r, scores[r], projected[r][1])


def split_kernel(query_ref, own_ref, core_ref):
    core = lax.axis_index("head")
    count = own_ref.shape[0]
    for k, to in enumerate((own_ref, core_ref)):
        for c in range(count):
            to[c] = query_ref[:, pl.ds(pl.multiple_of(((core ^ k) * count + c) * DH, DH), DH)]


def join_kernel(weight_ref, *rest):
    *pieces, out_ref = rest
    rows = weight_ref.shape[1]
    part = pieces[0].shape[1]
    out_ref[:, :rows, :] = weight_ref[...]
    for k, piece in enumerate(pieces):
        out_ref[:, rows + k * part : rows + (k + 1) * part, :] = piece[...]


def merge_kernel(back_ref, out_ref):
    count = back_ref.shape[0] // 4
    for n in range(4 * count):
        g, c, h = n // (2 * count), n // 2 % count, n % 2
        at = ((h * 2 + g) * count + c) * DH
        out_ref[:, at : at + DH] = back_ref[n]


def by_heads(queries, latents, image_span, image_owner, kv_weight, attn_gate):
    ctx_count = lax.axis_size("ctx")
    group = lax.axis_index("groups")
    place = lax.axis_index("ctx")
    core = lax.axis_index("head")
    part = queries.shape[0]
    width = kv_weight.shape[2]
    span = width // 2
    rows = kv_weight.shape[0]
    lat, depth = latents.shape[1:]
    images = image_span.shape[0]
    swap = [(0, 1), (1, 0)]
    smem = pl.BlockSpec(memory_space=pltpu.SMEM)
    vmem = pl.BlockSpec(memory_space=pltpu.VMEM)

    def across(x, turn):
        return lax.ppermute(x, "ctx", [(i, i ^ turn) for i in range(ctx_count)])

    share = lax.dynamic_slice_in_dim(latents[0], core * (depth // 2), depth // 2, 1)
    held = [share] + [across(share, 2 * k) for k in range(1, ctx_count // 2)]
    piece = jax.ShapeDtypeStruct((2 * ctx_count, part, DH), jnp.bfloat16)
    own, sent = pl.pallas_call(
        split_kernel,
        out_shape=[piece] * 2,
        in_specs=[vmem],
        out_specs=[vmem] * 2,
        compiler_params=pltpu.CompilerParams(vmem_limit_bytes=4 * 1024 * 1024),
    )(queries)
    came = lax.ppermute(sent, "head", swap)
    own, meta = lax.optimization_barrier((own, (image_span.T, image_owner[None, :])))
    meta = jnp.concatenate(meta, 0)
    meta_y = lax.ppermute(meta, "groups", swap)
    half = rows // 2
    weight = lax.dynamic_slice_in_dim(kv_weight, group * half, half, 0)
    weight = weight.reshape(half, 2, 2 * ctx_count, DH).transpose(2, 1, 0, 3)
    weight = weight.reshape(2 * ctx_count, 2 * half, DH)
    outgoing = pl.pallas_call(
        join_kernel,
        out_shape=jax.ShapeDtypeStruct((2 * ctx_count, 2 * half + 2 * part, DH), jnp.bfloat16),
        in_specs=[vmem] * 3,
        out_specs=vmem,
        compiler_params=pltpu.CompilerParams(vmem_limit_bytes=6 * 1024 * 1024),
    )(weight, own, came)
    outgoing, meta_y, *held = lax.optimization_barrier((outgoing, meta_y, *held))
    got = lax.all_to_all(outgoing, ("groups", "ctx"), split_axis=0, concat_axis=0, tiled=True)
    near = jnp.stack(held)
    near_y, far = lax.optimization_barrier((lax.ppermute(near, "groups", swap), across(near, 1)))
    cut = ctx_count // 4
    stores = [near, far, near_y, lax.ppermute(far[:cut], "groups", swap), across(near_y[cut:], 1)]
    stores += [lax.ppermute(x, "head", swap) for x in stores]
    gate = lax.dynamic_slice_in_dim(attn_gate.reshape(-1, DH), group * ctx_count + place, 1, 0)
    panel = pl.pallas_call(
        panel_kernel,
        out_shape=jax.ShapeDtypeStruct((2 * images * lat, depth), jnp.bfloat16),
        in_specs=[smem] * 2 + [vmem] * 10,
        out_specs=vmem,
        cost_estimate=pl.CostEstimate(flops=12_650_000_000, bytes_accessed=4 * 1024 * 1024, transcendentals=0),
        compiler_params=pltpu.CompilerParams(vmem_limit_bytes=8 * 1024 * 1024),
    )(meta, meta_y, *stores)
    gated = pl.pallas_call(
        functools.partial(attend_kernel, (ctx_count, rows, lat, part, images)),
        out_shape=jax.ShapeDtypeStruct((ctx_count * 4, part, DH), jnp.bfloat16),
        in_specs=[smem] * 2 + [vmem] * 3,
        out_specs=vmem,
        scratch_shapes=[pltpu.VMEM((depth, 2 * DH), jnp.bfloat16)],
        compiler_params=pltpu.CompilerParams(vmem_limit_bytes=16 * 1024 * 1024),
    )(meta, meta_y, gate, got, panel)
    every = ("groups", "ctx", "head")
    back = lax.all_to_all(gated, every, split_axis=0, concat_axis=0, tiled=True)
    return pl.pallas_call(
        merge_kernel,
        out_shape=jax.ShapeDtypeStruct((part, 2 * width), jnp.bfloat16),
        in_specs=[vmem],
        out_specs=vmem,
        compiler_params=pltpu.CompilerParams(vmem_limit_bytes=4 * 1024 * 1024),
    )(back)


def by_tokens(queries, latents, image_span, image_owner, kv_weight, attn_gate):
    ctx_count = lax.axis_size("ctx")
    rows = lax.all_to_all(queries, "head", split_axis=1, concat_axis=0, tiled=True)
    tok = rows.shape[0]
    width = rows.shape[1]
    lat = latents.shape[1]
    images = image_span.shape[0]
    query_norm = head_norm(rows.astype(jnp.float32), DH).astype(jnp.bfloat16)
    starts = image_span[:, 0]
    ends = image_span[:, 1]
    block_low = jnp.arange(ctx_count, dtype=jnp.int32) * tok
    meets = (starts[None, :] < (block_low + tok)[:, None]) & (ends[None, :] > block_low[:, None])
    counts = jnp.sum(meets.astype(jnp.int32), 1)
    firsts = jnp.sum((ends[None, :] <= block_low[:, None]).astype(jnp.int32), 1)
    slot_iota = jnp.arange(MAXIMG, dtype=jnp.int32)
    wanted = jnp.minimum(firsts[:, None] + slot_iota[None, :], images - 1)
    live = slot_iota[None, :] < counts[:, None]
    holders = image_owner[wanted]
    pieces = lax.all_to_all(latents, "ctx", split_axis=2, concat_axis=0, tiled=True)
    outgoing = jnp.where(live[:, :, None, None], pieces[holders], jnp.zeros((), jnp.bfloat16))
    panels = lax.all_to_all(outgoing, "ctx", split_axis=0, concat_axis=3, tiled=True)
    gathered = lax.all_gather(kv_weight, "ctx", axis=0, tiled=True)
    flat_weight = gathered.reshape(gathered.shape[0], 2 * width)
    both = jnp.dot(
        panels.reshape(MAXIMG * lat, panels.shape[3]),
        flat_weight,
        preferred_element_type=jnp.float32,
    )
    keys_out = head_norm(both[:, :width], DH).astype(jnp.bfloat16)
    values_out = both[:, width:].astype(jnp.bfloat16)
    mine = lax.axis_index("ctx")
    positions = mine * tok + jnp.arange(tok, dtype=jnp.int32)
    inside = (positions[:, None] >= starts[None, :]) & (positions[:, None] < ends[None, :])
    has_image = jnp.any(inside, 1)
    which = jnp.sum(jnp.where(inside, jnp.arange(images, dtype=jnp.int32)[None, :], 0), 1)
    my_first = jnp.sum((ends <= mine * tok).astype(jnp.int32))
    slot = which - my_first
    heads_here = width // DH
    query_heads = query_norm.reshape(tok, heads_here, DH)
    key_heads = keys_out.reshape(MAXIMG * lat, heads_here, DH)
    value_heads = values_out.reshape(MAXIMG * lat, heads_here, DH)
    scores = jnp.einsum(
        "thd,khd->thk", query_heads, key_heads, preferred_element_type=jnp.float32
    ) * DH ** (-0.5)
    owner_slot = jnp.arange(MAXIMG * lat, dtype=jnp.int32) // lat
    selected = (has_image[:, None] & (owner_slot[None, :] == slot[:, None])).astype(jnp.float32)
    weighted = jnp.exp(scores) * selected[:, None, :]
    total = (
        jnp.sum(weighted, -1, keepdims=True) + (1.0 - has_image.astype(jnp.float32))[:, None, None]
    )
    probs = (weighted / total).astype(jnp.bfloat16)
    attended = jnp.einsum("thk,khd->thd", probs, value_heads, preferred_element_type=jnp.float32)
    attended = attended.reshape(tok, width)
    gated = (jnp.tanh(attn_gate)[None, :] * attended).astype(jnp.bfloat16)
    return lax.all_to_all(gated, "head", split_axis=0, concat_axis=1, tiled=True)


def shards(*args):
    ctx_count = lax.axis_size("ctx")
    weight = args[4]
    pairs = lax.axis_size("groups") == 2 and lax.axis_size("head") == 2
    whole_heads = weight.shape[2] == 2 * ctx_count * DH
    whole_blocks = ctx_count % 4 == 0 and args[1].shape[2] % (2 * DH) == 0 and weight.shape[0] % 32 == 0
    if pairs and whole_heads and whole_blocks and ctx_count & (ctx_count - 1) == 0:
        return by_heads(*args)
    return by_tokens(*args)


def solution(mesh):
    placed = (
        P(("groups", "ctx", "head"), None),
        P(("groups", "ctx"), None, None),
        P("groups", None),
        P("groups"),
        P("ctx", None, "head"),
        P("head"),
    )
    return jax.shard_map(
        shards,
        mesh=mesh,
        in_specs=placed,
        out_specs=P(("groups", "ctx", "head"), None),
        check_vma=False,
    )
```

```python
import jax
import jax.numpy as jnp
from jax import lax
from jax.experimental import pallas as pl
from jax.experimental.pallas import tpu as pltpu
from jax.sharding import PartitionSpec as P

DH = 128
MAXIMG = 4


def head_norm(x, size):
    shaped = x.reshape(x.shape[:-1] + (x.shape[-1] // size, size))
    mean = jnp.mean(shaped, -1, keepdims=True)
    centered = shaped - mean
    spread = jnp.mean(centered * centered, -1, keepdims=True)
    return (centered * lax.rsqrt(spread + 1e-05)).reshape(x.shape)


def row_norm(x):
    centered = x - jnp.mean(x, -1, keepdims=True)
    spread = jnp.mean(centered * centered, -1, keepdims=True)
    return centered * lax.rsqrt(spread + 1e-05)


def panel_kernel(meta_ref, meta_y_ref, near, last, far, last_x, near_y, last_y, far_y, third, fourth, panel_ref):
    images = meta_ref.shape[1]
    lat = near.shape[1]
    place = lax.axis_index("ctx")

    def pick(few, one, slot):
        return jnp.where(slot < 3, few[jnp.minimum(slot, 2)], one[0])

    for r, meta in enumerate((meta_ref, meta_y_ref)):
        for i in range(images):
            turn = meta[2, i] ^ place
            slot = turn // 2
            if r == 0:
                one, other = pick(near, last, slot), pick(far, last_x, slot)
            else:
                one = pick(near_y, last_y, slot)
                other = jnp.where(slot == 2, third[0], fourth[0])
                other = jnp.where(slot < 2, far_y[jnp.minimum(slot, 1)], other)
            to = slice((r * images + i) * lat, (r * images + i + 1) * lat)
            panel_ref[to, :] = jnp.where(turn % 2 == 0, one, other)


def project_kernel(got_ref, other_ref, query_ref, weight_ref, partial_ref, weight):
    ctx_count, _, part, _ = query_ref.shape[1:]
    half = weight_ref.shape[0]
    rows = half // (ctx_count // 2)
    piece = rows // 2
    group = lax.axis_index("groups")
    core = lax.axis_index("head")
    for k, to_ref in enumerate((weight_ref, weight)):
        first = (core ^ k) * (ctx_count // 2)
        for s in range(ctx_count // 2):
            for g in range(2):
                at = s * rows + g * piece
                for n in range(2):
                    to_ref[at : at + piece, n * DH : (n + 1) * DH] = got_ref[
                        g * ctx_count + first + s, n * piece : (n + 1) * piece, :
                    ]
    partial_ref[...] = jnp.dot(other_ref[...], weight[...], preferred_element_type=jnp.float32)
    for r in range(2):
        query = got_ref[pl.ds((group ^ r) * ctx_count, ctx_count), rows : rows + 2 * part, :]
        query = query.reshape(ctx_count * 2 * part, DH).astype(jnp.float32)
        query_ref[r] = row_norm(query).astype(jnp.bfloat16).reshape(query_ref.shape[1:])


def attend_kernel(meta_ref, meta_y_ref, gate_ref, query_ref, weight_ref, partial_ref, own_ref, out_ref):
    ctx_count, _, part, _ = query_ref.shape[1:]
    images = meta_ref.shape[1]
    size = own_ref.shape[0] // 2
    lat = size // images
    count = ctx_count * 2 * part
    group = lax.axis_index("groups")
    core = lax.axis_index("head")
    metas = (meta_ref, meta_y_ref)
    queries = [query_ref[r].reshape(count, DH) for r in range(2)]
    gate = jnp.tanh(gate_ref[...])
    row = lax.broadcasted_iota(jnp.int32, (1, count), 1)
    block = row // part
    position = (block // 2 * 2 + (block % 2 ^ core)) * part + row % part

    def project(r):
        at = slice(r * size, (r + 1) * size)
        both = jnp.dot(own_ref[at, :], weight_ref[...], preferred_element_type=jnp.float32)
        both += partial_ref[at, :]
        return row_norm(both[:, :DH]).astype(jnp.bfloat16), both[:, DH:].astype(jnp.bfloat16)

    def score(r, keys):
        return lax.dot_general(
            keys, queries[r], (((1,), (1,)), ((), ())), preferred_element_type=jnp.float32
        ) * DH ** (-0.5)

    def finish(r, scores, values):
        weighted = []
        for i in range(images):
            inside = (position >= metas[r][0, i]) & (position < metas[r][1, i])
            weighted.append(jnp.where(inside, jnp.exp(scores[i * lat : (i + 1) * lat]), 0.0))
        total = sum(jnp.sum(w, 0, keepdims=True) for w in weighted)
        scale = 1.0 / jnp.where(total > 0.0, total, 1.0)
        probs = jnp.concatenate([(w * scale).astype(jnp.bfloat16) for w in weighted], 0)
        attended = lax.dot_general(
            values, probs, (((0,), (0,)), ((), ())), preferred_element_type=jnp.float32
        ).T
        gated = (gate * attended).astype(jnp.bfloat16).reshape(ctx_count, 2, part, DH)
        for c in range(ctx_count):
            for d in range(2):
                out_ref[((group ^ r) * ctx_count + c) * 2 + (core ^ d)] = gated[c, d]

    projected = [project(r) for r in range(2)]
    scores = [score(r, projected[r][0]) for r in range(2)]
    for r in range(2):
        finish(r, scores[r], projected[r][1])


def split_kernel(query_ref, own_ref, core_ref):
    core = lax.axis_index("head")
    count = own_ref.shape[0]
    for k, to in enumerate((own_ref, core_ref)):
        for c in range(count):
            to[c] = query_ref[:, pl.ds(pl.multiple_of(((core ^ k) * count + c) * DH, DH), DH)]


def join_kernel(weight_ref, *rest):
    *pieces, out_ref = rest
    rows = weight_ref.shape[1]
    part = pieces[0].shape[1]
    out_ref[:, :rows, :] = weight_ref[...]
    for k, piece in enumerate(pieces):
        out_ref[:, rows + k * part : rows + (k + 1) * part, :] = piece[...]


def merge_kernel(back_ref, out_ref):
    count = back_ref.shape[0] // 4
    for n in range(4 * count):
        g, c, h = n // (2 * count), n // 2 % count, n % 2
        at = ((h * 2 + g) * count + c) * DH
        out_ref[:, at : at + DH] = back_ref[n]


def by_heads(queries, latents, image_span, image_owner, kv_weight, attn_gate):
    ctx_count = lax.axis_size("ctx")
    group = lax.axis_index("groups")
    place = lax.axis_index("ctx")
    core = lax.axis_index("head")
    part = queries.shape[0]
    width = kv_weight.shape[2]
    span = width // 2
    rows = kv_weight.shape[0]
    lat, depth = latents.shape[1:]
    images = image_span.shape[0]
    swap = [(0, 1), (1, 0)]
    smem = pl.BlockSpec(memory_space=pltpu.SMEM)
    vmem = pl.BlockSpec(memory_space=pltpu.VMEM)

    def across(x, turn):
        return lax.ppermute(x, "ctx", [(i, i ^ turn) for i in range(ctx_count)])

    share = lax.dynamic_slice_in_dim(latents[0], core * (depth // 2), depth // 2, 1)
    share, meta = lax.optimization_barrier((share, (image_span.T, image_owner[None, :])))
    meta = jnp.concatenate(meta, 0)
    held = [share, across(share, 2), across(share, 4)]
    piece = jax.ShapeDtypeStruct((2 * ctx_count, part, DH), jnp.bfloat16)
    own, sent = pl.pallas_call(
        split_kernel,
        out_shape=[piece] * 2,
        in_specs=[vmem],
        out_specs=[vmem] * 2,
        compiler_params=pltpu.CompilerParams(vmem_limit_bytes=4 * 1024 * 1024),
    )(queries)
    came = lax.ppermute(sent, "head", swap)
    meta_y = lax.ppermute(meta, "groups", swap)
    half = rows // 2
    weight = lax.dynamic_slice_in_dim(kv_weight, group * half, half, 0)
    weight = weight.reshape(half, 2, 2 * ctx_count, DH).transpose(2, 1, 0, 3)
    weight = weight.reshape(2 * ctx_count, 2 * half, DH)
    outgoing = pl.pallas_call(
        join_kernel,
        out_shape=jax.ShapeDtypeStruct((2 * ctx_count, 2 * half + 2 * part, DH), jnp.bfloat16),
        in_specs=[vmem] * 3,
        out_specs=vmem,
        compiler_params=pltpu.CompilerParams(vmem_limit_bytes=6 * 1024 * 1024),
    )(weight, own, came)
    outgoing, meta_y, *held = lax.optimization_barrier((outgoing, meta_y, *held))
    got = lax.all_to_all(outgoing, ("groups", "ctx"), split_axis=0, concat_axis=0, tiled=True)
    near = jnp.stack(held)
    near_y, far, last = lax.optimization_barrier(
        (lax.ppermute(near, "groups", swap), across(near, 1), across(held[2], 2))
    )
    last = last[None]
    last_y = lax.ppermute(last, "groups", swap)
    last_x = across(last, 1)
    far_y = [lax.ppermute(far[:2], "groups", swap), across(near_y[2:], 1), across(last_y, 1)]
    stores = [near, last, far, last_x, near_y, last_y] + far_y
    stores += [lax.ppermute(x, "head", swap) for x in stores]
    gate = lax.dynamic_slice_in_dim(attn_gate.reshape(-1, DH), group * ctx_count + place, 1, 0)
    panels = [
        pl.pallas_call(
            panel_kernel,
            out_shape=jax.ShapeDtypeStruct((2 * images * lat, depth // 2), jnp.bfloat16),
            in_specs=[smem] * 2 + [vmem] * 9,
            out_specs=vmem,
            cost_estimate=pl.CostEstimate(flops=8050000000, bytes_accessed=2 * 1024 * 1024, transcendentals=0),
            compiler_params=pltpu.CompilerParams(vmem_limit_bytes=6 * 1024 * 1024),
        )(meta, meta_y, *stores[9 * k : 9 * k + 9])
        for k in range(2)
    ]
    query, weight, partial = pl.pallas_call(
        project_kernel,
        out_shape=[
            jax.ShapeDtypeStruct((2, ctx_count, 2, part, DH), jnp.bfloat16),
            jax.ShapeDtypeStruct((depth // 2, 2 * DH), jnp.bfloat16),
            jax.ShapeDtypeStruct((2 * images * lat, 2 * DH), jnp.float32),
        ],
        in_specs=[vmem] * 2,
        out_specs=[vmem] * 3,
        scratch_shapes=[pltpu.VMEM((depth // 2, 2 * DH), jnp.bfloat16)],
        cost_estimate=pl.CostEstimate(flops=2 * 10**8, bytes_accessed=16000000, transcendentals=0),
        compiler_params=pltpu.CompilerParams(vmem_limit_bytes=8 * 1024 * 1024),
    )(got, panels[1])
    gated = pl.pallas_call(
        attend_kernel,
        out_shape=jax.ShapeDtypeStruct((ctx_count * 4, part, DH), jnp.bfloat16),
        in_specs=[smem] * 2 + [vmem] * 5,
        out_specs=vmem,
        cost_estimate=pl.CostEstimate(flops=20000000000, bytes_accessed=4 * 1024 * 1024, transcendentals=0),
        compiler_params=pltpu.CompilerParams(vmem_limit_bytes=16 * 1024 * 1024),
    )(meta, meta_y, gate, query, weight, partial, panels[0])
    every = ("groups", "ctx", "head")
    back = lax.all_to_all(gated, every, split_axis=0, concat_axis=0, tiled=True)
    return pl.pallas_call(
        merge_kernel,
        out_shape=jax.ShapeDtypeStruct((part, 2 * width), jnp.bfloat16),
        in_specs=[vmem],
        out_specs=vmem,
        compiler_params=pltpu.CompilerParams(vmem_limit_bytes=4 * 1024 * 1024),
    )(back)


def by_tokens(queries, latents, image_span, image_owner, kv_weight, attn_gate):
    ctx_count = lax.axis_size("ctx")
    rows = lax.all_to_all(queries, "head", split_axis=1, concat_axis=0, tiled=True)
    tok = rows.shape[0]
    width = rows.shape[1]
    lat = latents.shape[1]
    images = image_span.shape[0]
    query_norm = head_norm(rows.astype(jnp.float32), DH).astype(jnp.bfloat16)
    starts = image_span[:, 0]
    ends = image_span[:, 1]
    block_low = jnp.arange(ctx_count, dtype=jnp.int32) * tok
    meets = (starts[None, :] < (block_low + tok)[:, None]) & (ends[None, :] > block_low[:, None])
    counts = jnp.sum(meets.astype(jnp.int32), 1)
    firsts = jnp.sum((ends[None, :] <= block_low[:, None]).astype(jnp.int32), 1)
    slot_iota = jnp.arange(MAXIMG, dtype=jnp.int32)
    wanted = jnp.minimum(firsts[:, None] + slot_iota[None, :], images - 1)
    live = slot_iota[None, :] < counts[:, None]
    holders = image_owner[wanted]
    pieces = lax.all_to_all(latents, "ctx", split_axis=2, concat_axis=0, tiled=True)
    outgoing = jnp.where(live[:, :, None, None], pieces[holders], jnp.zeros((), jnp.bfloat16))
    panels = lax.all_to_all(outgoing, "ctx", split_axis=0, concat_axis=3, tiled=True)
    gathered = lax.all_gather(kv_weight, "ctx", axis=0, tiled=True)
    flat_weight = gathered.reshape(gathered.shape[0], 2 * width)
    both = jnp.dot(
        panels.reshape(MAXIMG * lat, panels.shape[3]),
        flat_weight,
        preferred_element_type=jnp.float32,
    )
    keys_out = head_norm(both[:, :width], DH).astype(jnp.bfloat16)
    values_out = both[:, width:].astype(jnp.bfloat16)
    mine = lax.axis_index("ctx")
    positions = mine * tok + jnp.arange(tok, dtype=jnp.int32)
    inside = (positions[:, None] >= starts[None, :]) & (positions[:, None] < ends[None, :])
    has_image = jnp.any(inside, 1)
    which = jnp.sum(jnp.where(inside, jnp.arange(images, dtype=jnp.int32)[None, :], 0), 1)
    my_first = jnp.sum((ends <= mine * tok).astype(jnp.int32))
    slot = which - my_first
    heads_here = width // DH
    query_heads = query_norm.reshape(tok, heads_here, DH)
    key_heads = keys_out.reshape(MAXIMG * lat, heads_here, DH)
    value_heads = values_out.reshape(MAXIMG * lat, heads_here, DH)
    scores = jnp.einsum(
        "thd,khd->thk", query_heads, key_heads, preferred_element_type=jnp.float32
    ) * DH ** (-0.5)
    owner_slot = jnp.arange(MAXIMG * lat, dtype=jnp.int32) // lat
    selected = (has_image[:, None] & (owner_slot[None, :] == slot[:, None])).astype(jnp.float32)
    weighted = jnp.exp(scores) * selected[:, None, :]
    total = (
        jnp.sum(weighted, -1, keepdims=True) + (1.0 - has_image.astype(jnp.float32))[:, None, None]
    )
    probs = (weighted / total).astype(jnp.bfloat16)
    attended = jnp.einsum("thk,khd->thd", probs, value_heads, preferred_element_type=jnp.float32)
    attended = attended.reshape(tok, width)
    gated = (jnp.tanh(attn_gate)[None, :] * attended).astype(jnp.bfloat16)
    return lax.all_to_all(gated, "head", split_axis=0, concat_axis=1, tiled=True)


def shards(*args):
    ctx_count = lax.axis_size("ctx")
    weight = args[4]
    pairs = lax.axis_size("groups") == 2 and lax.axis_size("head") == 2
    whole_heads = weight.shape[2] == 2 * ctx_count * DH
    whole_blocks = ctx_count == 8 and args[1].shape[2] % (2 * DH) == 0 and weight.shape[0] % 32 == 0
    if pairs and whole_heads and whole_blocks and ctx_count & (ctx_count - 1) == 0:
        return by_heads(*args)
    return by_tokens(*args)


def solution(mesh):
    placed = (
        P(("groups", "ctx", "head"), None),
        P(("groups", "ctx"), None, None),
        P("groups", None),
        P("groups"),
        P("ctx", None, "head"),
        P("head"),
    )
    return jax.shard_map(
        shards,
        mesh=mesh,
        in_specs=placed,
        out_specs=P(("groups", "ctx", "head"), None),
        check_vma=False,
    )
```

```python
import jax
import jax.numpy as jnp
from jax import lax
from jax.experimental import pallas as pl
from jax.experimental.pallas import tpu as pltpu
from jax.sharding import PartitionSpec as P

DH = 128
MAXIMG = 4


def head_norm(x, size):
    shaped = x.reshape(x.shape[:-1] + (x.shape[-1] // size, size))
    mean = jnp.mean(shaped, -1, keepdims=True)
    centered = shaped - mean
    spread = jnp.mean(centered * centered, -1, keepdims=True)
    return (centered * lax.rsqrt(spread + 1e-05)).reshape(x.shape)


def row_norm(x):
    centered = x - jnp.mean(x, -1, keepdims=True)
    spread = jnp.mean(centered * centered, -1, keepdims=True)
    return centered * lax.rsqrt(spread + 1e-05)


def panel_kernel(meta_ref, meta_y_ref, near, last, far, last_x, near_y, last_y, far_y, third, fourth, panel_ref):
    images = meta_ref.shape[1]
    lat = near.shape[1]
    place = lax.axis_index("ctx")

    def pick(few, one, slot):
        return jnp.where(slot < 3, few[jnp.minimum(slot, 2)], one[0])

    for r, meta in enumerate((meta_ref, meta_y_ref)):
        for i in range(images):
            turn = meta[2, i] ^ place
            slot = turn // 2
            if r == 0:
                one, other = pick(near, last, slot), pick(far, last_x, slot)
            else:
                one = pick(near_y, last_y, slot)
                other = jnp.where(slot == 2, third[0], fourth[0])
                other = jnp.where(slot < 2, far_y[jnp.minimum(slot, 1)], other)
            to = slice((r * images + i) * lat, (r * images + i + 1) * lat)
            panel_ref[to, :] = jnp.where(turn % 2 == 0, one, other)


def project_kernel(got_ref, other_ref, query_ref, weight_ref, partial_ref, weight):
    ctx_count, _, part, _ = query_ref.shape[1:]
    half = weight_ref.shape[0]
    rows = half // (ctx_count // 2)
    piece = rows // 2
    group = lax.axis_index("groups")
    core = lax.axis_index("head")
    for k, to_ref in enumerate((weight_ref, weight)):
        first = (core ^ k) * (ctx_count // 2)
        for s in range(ctx_count // 2):
            for g in range(2):
                at = s * rows + g * piece
                for n in range(2):
                    to_ref[at : at + piece, n * DH : (n + 1) * DH] = got_ref[
                        g * ctx_count + first + s, n * piece : (n + 1) * piece, :
                    ]
    partial_ref[...] = jnp.dot(other_ref[...], weight[...], preferred_element_type=jnp.float32)
    for r in range(2):
        query = got_ref[pl.ds((group ^ r) * ctx_count, ctx_count), rows : rows + 2 * part, :]
        query = query.reshape(ctx_count * 2 * part, DH).astype(jnp.float32)
        query_ref[r] = row_norm(query).astype(jnp.bfloat16).reshape(query_ref.shape[1:])


def attend_kernel(meta_ref, meta_y_ref, gate_ref, query_ref, weight_ref, partial_ref, own_ref, out_ref):
    ctx_count, _, part, _ = query_ref.shape[1:]
    images = meta_ref.shape[1]
    size = own_ref.shape[0] // 2
    lat = size // images
    count = ctx_count * 2 * part
    group = lax.axis_index("groups")
    core = lax.axis_index("head")
    metas = (meta_ref, meta_y_ref)
    queries = [query_ref[r].reshape(count, DH) for r in range(2)]
    gate = jnp.tanh(gate_ref[...])
    row = lax.broadcasted_iota(jnp.int32, (1, count), 1)
    block = row // part
    position = (block // 2 * 2 + (block % 2 ^ core)) * part + row % part

    def project(r):
        at = slice(r * size, (r + 1) * size)
        both = jnp.dot(own_ref[at, :], weight_ref[...], preferred_element_type=jnp.float32)
        both += partial_ref[at, :]
        return row_norm(both[:, :DH]).astype(jnp.bfloat16), both[:, DH:].astype(jnp.bfloat16)

    def score(r, keys):
        return lax.dot_general(
            keys, queries[r], (((1,), (1,)), ((), ())), preferred_element_type=jnp.float32
        ) * DH ** (-0.5)

    def finish(r, scores, values):
        weighted = []
        for i in range(images):
            inside = (position >= metas[r][0, i]) & (position < metas[r][1, i])
            weighted.append(jnp.where(inside, jnp.exp(scores[i * lat : (i + 1) * lat]), 0.0))
        total = sum(jnp.sum(w, 0, keepdims=True) for w in weighted)
        scale = 1.0 / jnp.where(total > 0.0, total, 1.0)
        probs = jnp.concatenate([(w * scale).astype(jnp.bfloat16) for w in weighted], 0)
        attended = lax.dot_general(
            values, probs, (((0,), (0,)), ((), ())), preferred_element_type=jnp.float32
        ).T
        gated = (gate * attended).astype(jnp.bfloat16).reshape(ctx_count, 2, part, DH)
        for c in range(ctx_count):
            for d in range(2):
                out_ref[((group ^ r) * ctx_count + c) * 2 + (core ^ d)] = gated[c, d]

    projected = [project(r) for r in range(2)]
    scores = [score(r, projected[r][0]) for r in range(2)]
    for r in range(2):
        finish(r, scores[r], projected[r][1])


def split_kernel(query_ref, own_ref, core_ref):
    core = lax.axis_index("head")
    count = own_ref.shape[0]
    for k, to in enumerate((own_ref, core_ref)):
        for c in range(count):
            to[c] = query_ref[:, pl.ds(pl.multiple_of(((core ^ k) * count + c) * DH, DH), DH)]


def join_kernel(weight_ref, *rest):
    *pieces, out_ref = rest
    rows = weight_ref.shape[1]
    part = pieces[0].shape[1]
    out_ref[:, :rows, :] = weight_ref[...]
    for k, piece in enumerate(pieces):
        out_ref[:, rows + k * part : rows + (k + 1) * part, :] = piece[...]


def merge_kernel(back_ref, out_ref):
    count = back_ref.shape[0] // 4
    for n in range(4 * count):
        g, c, h = n // (2 * count), n // 2 % count, n % 2
        at = ((h * 2 + g) * count + c) * DH
        out_ref[:, at : at + DH] = back_ref[n]


def by_heads(queries, latents, image_span, image_owner, kv_weight, attn_gate):
    ctx_count = lax.axis_size("ctx")
    group = lax.axis_index("groups")
    place = lax.axis_index("ctx")
    core = lax.axis_index("head")
    part = queries.shape[0]
    width = kv_weight.shape[2]
    span = width // 2
    rows = kv_weight.shape[0]
    lat, depth = latents.shape[1:]
    images = image_span.shape[0]
    swap = [(0, 1), (1, 0)]
    smem = pl.BlockSpec(memory_space=pltpu.SMEM)
    vmem = pl.BlockSpec(memory_space=pltpu.VMEM)

    def across(x, turn):
        return lax.ppermute(x, "ctx", [(i, i ^ turn) for i in range(ctx_count)])

    share = lax.dynamic_slice_in_dim(latents[0], core * (depth // 2), depth // 2, 1)
    share, meta = lax.optimization_barrier((share, (image_span.T, image_owner[None, :])))
    meta = jnp.concatenate(meta, 0)
    held = [share, across(share, 2), across(share, 4)]
    piece = jax.ShapeDtypeStruct((2 * ctx_count, part, DH), jnp.bfloat16)
    own, sent = pl.pallas_call(
        split_kernel,
        out_shape=[piece] * 2,
        in_specs=[vmem],
        out_specs=[vmem] * 2,
        compiler_params=pltpu.CompilerParams(vmem_limit_bytes=4 * 1024 * 1024),
    )(queries)
    came = lax.ppermute(sent, "head", swap)
    meta_y = lax.ppermute(meta, "groups", swap)
    half = rows // 2
    weight = lax.dynamic_slice_in_dim(kv_weight, group * half, half, 0)
    weight = weight.reshape(half, 2, 2 * ctx_count, DH).transpose(2, 1, 0, 3)
    weight = weight.reshape(2 * ctx_count, 2 * half, DH)
    outgoing = pl.pallas_call(
        join_kernel,
        out_shape=jax.ShapeDtypeStruct((2 * ctx_count, 2 * half + 2 * part, DH), jnp.bfloat16),
        in_specs=[vmem] * 3,
        out_specs=vmem,
        compiler_params=pltpu.CompilerParams(vmem_limit_bytes=6 * 1024 * 1024),
    )(weight, own, came)
    outgoing, meta_y, *held = lax.optimization_barrier((outgoing, meta_y, *held))
    got = lax.all_to_all(outgoing, ("groups", "ctx"), split_axis=0, concat_axis=0, tiled=True)
    near = jnp.stack(held)
    near_y, far, last = lax.optimization_barrier(
        (lax.ppermute(near, "groups", swap), across(near, 1), across(held[2], 2))
    )
    last = last[None]
    last_y = lax.ppermute(last, "groups", swap)
    last_x = across(last, 1)
    far_y = [across(near_y[:2], 1), lax.ppermute(far[2:], "groups", swap), lax.ppermute(last_x, "groups", swap)]
    stores = [near, last, far, last_x, near_y, last_y] + far_y
    stores += [lax.ppermute(x, "head", swap) for x in stores]
    gate = lax.dynamic_slice_in_dim(attn_gate.reshape(-1, DH), group * ctx_count + place, 1, 0)
    panels = [
        pl.pallas_call(
            panel_kernel,
            out_shape=jax.ShapeDtypeStruct((2 * images * lat, depth // 2), jnp.bfloat16),
            in_specs=[smem] * 2 + [vmem] * 9,
            out_specs=vmem,
            cost_estimate=pl.CostEstimate(flops=8_050_000_000, bytes_accessed=2 * 1024 * 1024, transcendentals=0),
            compiler_params=pltpu.CompilerParams(vmem_limit_bytes=6 * 1024 * 1024),
        )(meta, meta_y, *stores[9 * k : 9 * k + 9])
        for k in range(2)
    ]
    query, weight, partial = pl.pallas_call(
        project_kernel,
        out_shape=[
            jax.ShapeDtypeStruct((2, ctx_count, 2, part, DH), jnp.bfloat16),
            jax.ShapeDtypeStruct((depth // 2, 2 * DH), jnp.bfloat16),
            jax.ShapeDtypeStruct((2 * images * lat, 2 * DH), jnp.float32),
        ],
        in_specs=[vmem] * 2,
        out_specs=[vmem] * 3,
        scratch_shapes=[pltpu.VMEM((depth // 2, 2 * DH), jnp.bfloat16)],
        cost_estimate=pl.CostEstimate(flops=2 * 10**8, bytes_accessed=16_000_000, transcendentals=0),
        compiler_params=pltpu.CompilerParams(vmem_limit_bytes=8 * 1024 * 1024),
    )(got, panels[1])
    gated = pl.pallas_call(
        attend_kernel,
        out_shape=jax.ShapeDtypeStruct((ctx_count * 4, part, DH), jnp.bfloat16),
        in_specs=[smem] * 2 + [vmem] * 5,
        out_specs=vmem,
        cost_estimate=pl.CostEstimate(flops=20_000_000_000, bytes_accessed=4 * 1024 * 1024, transcendentals=0),
        compiler_params=pltpu.CompilerParams(vmem_limit_bytes=16 * 1024 * 1024),
    )(meta, meta_y, gate, query, weight, partial, panels[0])
    every = ("groups", "ctx", "head")
    back = lax.all_to_all(gated, every, split_axis=0, concat_axis=0, tiled=True)
    return pl.pallas_call(
        merge_kernel,
        out_shape=jax.ShapeDtypeStruct((part, 2 * width), jnp.bfloat16),
        in_specs=[vmem],
        out_specs=vmem,
        compiler_params=pltpu.CompilerParams(vmem_limit_bytes=4 * 1024 * 1024),
    )(back)


def by_tokens(queries, latents, image_span, image_owner, kv_weight, attn_gate):
    ctx_count = lax.axis_size("ctx")
    rows = lax.all_to_all(queries, "head", split_axis=1, concat_axis=0, tiled=True)
    tok = rows.shape[0]
    width = rows.shape[1]
    lat = latents.shape[1]
    images = image_span.shape[0]
    query_norm = head_norm(rows.astype(jnp.float32), DH).astype(jnp.bfloat16)
    starts = image_span[:, 0]
    ends = image_span[:, 1]
    block_low = jnp.arange(ctx_count, dtype=jnp.int32) * tok
    meets = (starts[None, :] < (block_low + tok)[:, None]) & (ends[None, :] > block_low[:, None])
    counts = jnp.sum(meets.astype(jnp.int32), 1)
    firsts = jnp.sum((ends[None, :] <= block_low[:, None]).astype(jnp.int32), 1)
    slot_iota = jnp.arange(MAXIMG, dtype=jnp.int32)
    wanted = jnp.minimum(firsts[:, None] + slot_iota[None, :], images - 1)
    live = slot_iota[None, :] < counts[:, None]
    holders = image_owner[wanted]
    pieces = lax.all_to_all(latents, "ctx", split_axis=2, concat_axis=0, tiled=True)
    outgoing = jnp.where(live[:, :, None, None], pieces[holders], jnp.zeros((), jnp.bfloat16))
    panels = lax.all_to_all(outgoing, "ctx", split_axis=0, concat_axis=3, tiled=True)
    gathered = lax.all_gather(kv_weight, "ctx", axis=0, tiled=True)
    flat_weight = gathered.reshape(gathered.shape[0], 2 * width)
    both = jnp.dot(
        panels.reshape(MAXIMG * lat, panels.shape[3]),
        flat_weight,
        preferred_element_type=jnp.float32,
    )
    keys_out = head_norm(both[:, :width], DH).astype(jnp.bfloat16)
    values_out = both[:, width:].astype(jnp.bfloat16)
    mine = lax.axis_index("ctx")
    positions = mine * tok + jnp.arange(tok, dtype=jnp.int32)
    inside = (positions[:, None] >= starts[None, :]) & (positions[:, None] < ends[None, :])
    has_image = jnp.any(inside, 1)
    which = jnp.sum(jnp.where(inside, jnp.arange(images, dtype=jnp.int32)[None, :], 0), 1)
    my_first = jnp.sum((ends <= mine * tok).astype(jnp.int32))
    slot = which - my_first
    heads_here = width // DH
    query_heads = query_norm.reshape(tok, heads_here, DH)
    key_heads = keys_out.reshape(MAXIMG * lat, heads_here, DH)
    value_heads = values_out.reshape(MAXIMG * lat, heads_here, DH)
    scores = jnp.einsum(
        "thd,khd->thk", query_heads, key_heads, preferred_element_type=jnp.float32
    ) * DH ** (-0.5)
    owner_slot = jnp.arange(MAXIMG * lat, dtype=jnp.int32) // lat
    selected = (has_image[:, None] & (owner_slot[None, :] == slot[:, None])).astype(jnp.float32)
    weighted = jnp.exp(scores) * selected[:, None, :]
    total = (
        jnp.sum(weighted, -1, keepdims=True) + (1.0 - has_image.astype(jnp.float32))[:, None, None]
    )
    probs = (weighted / total).astype(jnp.bfloat16)
    attended = jnp.einsum("thk,khd->thd", probs, value_heads, preferred_element_type=jnp.float32)
    attended = attended.reshape(tok, width)
    gated = (jnp.tanh(attn_gate)[None, :] * attended).astype(jnp.bfloat16)
    return lax.all_to_all(gated, "head", split_axis=0, concat_axis=1, tiled=True)


def shards(*args):
    ctx_count = lax.axis_size("ctx")
    weight = args[4]
    pairs = lax.axis_size("groups") == 2 and lax.axis_size("head") == 2
    whole_heads = weight.shape[2] == 2 * ctx_count * DH
    whole_blocks = ctx_count == 8 and args[1].shape[2] % (2 * DH) == 0 and weight.shape[0] % 32 == 0
    if pairs and whole_heads and whole_blocks and ctx_count & (ctx_count - 1) == 0:
        return by_heads(*args)
    return by_tokens(*args)


def solution(mesh):
    placed = (
        P(("groups", "ctx", "head"), None),
        P(("groups", "ctx"), None, None),
        P("groups", None),
        P("groups"),
        P("ctx", None, "head"),
        P("head"),
    )
    return jax.shard_map(
        shards,
        mesh=mesh,
        in_specs=placed,
        out_specs=P(("groups", "ctx", "head"), None),
        check_vma=False,
    )
```

```python
import jax
import jax.numpy as jnp
from jax import lax
from jax.experimental import pallas as pl
from jax.experimental.pallas import tpu as pltpu
from jax.sharding import PartitionSpec as P

DH = 128
MAXIMG = 4


def head_norm(x, size):
    shaped = x.reshape(x.shape[:-1] + (x.shape[-1] // size, size))
    mean = jnp.mean(shaped, -1, keepdims=True)
    centered = shaped - mean
    spread = jnp.mean(centered * centered, -1, keepdims=True)
    return (centered * lax.rsqrt(spread + 1e-05)).reshape(x.shape)


def row_norm(x):
    centered = x - jnp.mean(x, -1, keepdims=True)
    spread = jnp.mean(centered * centered, -1, keepdims=True)
    return centered * lax.rsqrt(spread + 1e-05)


def place_images(meta_ref, meta_y_ref, near, last, far, last_x, near_y, last_y, far_y, third, fourth, put):
    images = meta_ref.shape[1]
    lat = near.shape[1]
    place = lax.axis_index("ctx")

    def pick(few, one, slot):
        return jnp.where(slot < 3, few[jnp.minimum(slot, 2)], one[0])

    for r, meta in enumerate((meta_ref, meta_y_ref)):
        for i in range(images):
            turn = meta[2, i] ^ place
            slot = turn // 2
            if r == 0:
                one, other = pick(near, last, slot), pick(far, last_x, slot)
            else:
                one = pick(near_y, last_y, slot)
                other = jnp.where(slot == 2, third[0], fourth[0])
                other = jnp.where(slot < 2, far_y[jnp.minimum(slot, 1)], other)
            to = slice((r * images + i) * lat, (r * images + i + 1) * lat)
            put(to, jnp.where(turn % 2 == 0, one, other))


def own_kernel(meta_ref, meta_y_ref, *rest):
    *stores, first_ref, late_ref = rest
    cut = first_ref.shape[1]

    def put(to, image):
        first_ref[to, :] = image[:, :cut]
        late_ref[to, :] = image[:, cut:]

    place_images(meta_ref, meta_y_ref, *stores, put)


def kept_kernel(meta_ref, meta_y_ref, *rest):
    *stores, first_ref, kept_ref = rest
    half = stores[0].shape[2]

    def put(to, image):
        kept_ref[to, :half] = image

    place_images(meta_ref, meta_y_ref, *stores, put)
    kept_ref[:, half:] = first_ref[...]


def project_kernel(got_ref, kept_ref, query_ref, weight_ref, partial_ref, weight):
    ctx_count, _, part, _ = query_ref.shape[1:]
    half = weight.shape[0] // 2
    rows = half // (ctx_count // 2)
    piece = rows // 2
    group = lax.axis_index("groups")
    core = lax.axis_index("head")
    for k in range(2):
        first = (core ^ 1 ^ k) * (ctx_count // 2)
        for s in range(ctx_count // 2):
            for g in range(2):
                at = k * half + s * rows + g * piece
                for n in range(2):
                    weight[at : at + piece, n * DH : (n + 1) * DH] = got_ref[
                        g * ctx_count + first + s, n * piece : (n + 1) * piece, :
                    ]
    cut = kept_ref.shape[1]
    partial_ref[...] = jnp.dot(kept_ref[...], weight[:cut, :], preferred_element_type=jnp.float32)
    weight_ref[...] = weight[cut:, :]
    for r in range(2):
        query = got_ref[pl.ds((group ^ r) * ctx_count, ctx_count), rows : rows + 2 * part, :]
        query = query.reshape(ctx_count * 2 * part, DH).astype(jnp.float32)
        query_ref[r] = row_norm(query).astype(jnp.bfloat16).reshape(query_ref.shape[1:])


def attend_kernel(meta_ref, meta_y_ref, gate_ref, query_ref, weight_ref, partial_ref, late_ref, out_ref):
    ctx_count, _, part, _ = query_ref.shape[1:]
    images = meta_ref.shape[1]
    size = late_ref.shape[0] // 2
    lat = size // images
    count = ctx_count * 2 * part
    group = lax.axis_index("groups")
    core = lax.axis_index("head")
    metas = (meta_ref, meta_y_ref)
    queries = [query_ref[r].reshape(count, DH) for r in range(2)]
    gate = jnp.tanh(gate_ref[...])
    row = lax.broadcasted_iota(jnp.int32, (1, count), 1)
    block = row // part
    position = (block // 2 * 2 + (block % 2 ^ core)) * part + row % part

    def project(r):
        at = slice(r * size, (r + 1) * size)
        both = jnp.dot(late_ref[at, :], weight_ref[...], preferred_element_type=jnp.float32)
        both += partial_ref[at, :]
        return row_norm(both[:, :DH]).astype(jnp.bfloat16), both[:, DH:].astype(jnp.bfloat16)

    def score(r, keys):
        return lax.dot_general(
            keys, queries[r], (((1,), (1,)), ((), ())), preferred_element_type=jnp.float32
        ) * DH ** (-0.5)

    def finish(r, scores, values):
        weighted = []
        for i in range(images):
            inside = (position >= metas[r][0, i]) & (position < metas[r][1, i])
            weighted.append(jnp.where(inside, jnp.exp(scores[i * lat : (i + 1) * lat]), 0.0))
        total = sum(jnp.sum(w, 0, keepdims=True) for w in weighted)
        scale = 1.0 / jnp.where(total > 0.0, total, 1.0)
        probs = jnp.concatenate([(w * scale).astype(jnp.bfloat16) for w in weighted], 0)
        attended = lax.dot_general(
            values, probs, (((0,), (0,)), ((), ())), preferred_element_type=jnp.float32
        ).T
        gated = (gate * attended).astype(jnp.bfloat16).reshape(ctx_count, 2, part, DH)
        for c in range(ctx_count):
            for d in range(2):
                out_ref[((group ^ r) * ctx_count + c) * 2 + (core ^ d)] = gated[c, d]

    projected = [project(r) for r in range(2)]
    scores = [score(r, projected[r][0]) for r in range(2)]
    for r in range(2):
        finish(r, scores[r], projected[r][1])


def split_kernel(query_ref, own_ref, core_ref):
    core = lax.axis_index("head")
    count = own_ref.shape[0]
    for k, to in enumerate((own_ref, core_ref)):
        for c in range(count):
            to[c] = query_ref[:, pl.ds(pl.multiple_of(((core ^ k) * count + c) * DH, DH), DH)]


def join_kernel(weight_ref, *rest):
    *pieces, out_ref = rest
    rows = weight_ref.shape[1]
    part = pieces[0].shape[1]
    out_ref[:, :rows, :] = weight_ref[...]
    for k, piece in enumerate(pieces):
        out_ref[:, rows + k * part : rows + (k + 1) * part, :] = piece[...]


def merge_kernel(back_ref, out_ref):
    count = back_ref.shape[0] // 4
    for n in range(4 * count):
        g, c, h = n // (2 * count), n // 2 % count, n % 2
        at = ((h * 2 + g) * count + c) * DH
        out_ref[:, at : at + DH] = back_ref[n]


def by_heads(queries, latents, image_span, image_owner, kv_weight, attn_gate):
    ctx_count = lax.axis_size("ctx")
    group = lax.axis_index("groups")
    place = lax.axis_index("ctx")
    core = lax.axis_index("head")
    part = queries.shape[0]
    width = kv_weight.shape[2]
    span = width // 2
    rows = kv_weight.shape[0]
    lat, depth = latents.shape[1:]
    images = image_span.shape[0]
    swap = [(0, 1), (1, 0)]
    smem = pl.BlockSpec(memory_space=pltpu.SMEM)
    vmem = pl.BlockSpec(memory_space=pltpu.VMEM)

    def across(x, turn):
        return lax.ppermute(x, "ctx", [(i, i ^ turn) for i in range(ctx_count)])

    share = lax.dynamic_slice_in_dim(latents[0], core * (depth // 2), depth // 2, 1)
    share, meta = lax.optimization_barrier((share, (image_span.T, image_owner[None, :])))
    meta = jnp.concatenate(meta, 0)
    held = [share, across(share, 2), across(share, 4)]
    piece = jax.ShapeDtypeStruct((2 * ctx_count, part, DH), jnp.bfloat16)
    own, sent = pl.pallas_call(
        split_kernel,
        out_shape=[piece] * 2,
        in_specs=[vmem],
        out_specs=[vmem] * 2,
        compiler_params=pltpu.CompilerParams(vmem_limit_bytes=4 * 1024 * 1024),
    )(queries)
    came = lax.ppermute(sent, "head", swap)
    meta_y = lax.ppermute(meta, "groups", swap)
    half = rows // 2
    weight = lax.dynamic_slice_in_dim(kv_weight, group * half, half, 0)
    weight = weight.reshape(half, 2, 2 * ctx_count, DH).transpose(2, 1, 0, 3)
    weight = weight.reshape(2 * ctx_count, 2 * half, DH)
    outgoing = pl.pallas_call(
        join_kernel,
        out_shape=jax.ShapeDtypeStruct((2 * ctx_count, 2 * half + 2 * part, DH), jnp.bfloat16),
        in_specs=[vmem] * 3,
        out_specs=vmem,
        compiler_params=pltpu.CompilerParams(vmem_limit_bytes=6 * 1024 * 1024),
    )(weight, own, came)
    outgoing, meta_y, *held = lax.optimization_barrier((outgoing, meta_y, *held))
    got = lax.all_to_all(outgoing, ("groups", "ctx"), split_axis=0, concat_axis=0, tiled=True)
    near = jnp.stack(held)
    near_y, far, last = lax.optimization_barrier(
        (lax.ppermute(near, "groups", swap), across(near, 1), across(held[2], 2))
    )
    last = last[None]
    last_y = lax.ppermute(last, "groups", swap)
    last_x = across(last, 1)
    far_y = [across(near_y[:2], 1), lax.ppermute(far[2:], "groups", swap), lax.ppermute(last_x, "groups", swap)]
    stores = [near, last, far, last_x, near_y, last_y] + far_y
    stores += [lax.ppermute(x, "head", swap) for x in stores]
    gate = lax.dynamic_slice_in_dim(attn_gate.reshape(-1, DH), group * ctx_count + place, 1, 0)
    late = 3 * DH
    size = 2 * images * lat
    first, last_columns = pl.pallas_call(
        own_kernel,
        out_shape=[
            jax.ShapeDtypeStruct((size, depth // 2 - late), jnp.bfloat16),
            jax.ShapeDtypeStruct((size, late), jnp.bfloat16),
        ],
        in_specs=[smem] * 2 + [vmem] * 9,
        out_specs=[vmem] * 2,
        cost_estimate=pl.CostEstimate(flops=8_050_000_000, bytes_accessed=2 * 1024 * 1024, transcendentals=0),
        compiler_params=pltpu.CompilerParams(vmem_limit_bytes=6 * 1024 * 1024),
    )(meta, meta_y, *stores[:9])
    kept = pl.pallas_call(
        kept_kernel,
        out_shape=jax.ShapeDtypeStruct((size, depth - late), jnp.bfloat16),
        in_specs=[smem] * 2 + [vmem] * 10,
        out_specs=vmem,
        cost_estimate=pl.CostEstimate(flops=8_050_000_000, bytes_accessed=2 * 1024 * 1024, transcendentals=0),
        compiler_params=pltpu.CompilerParams(vmem_limit_bytes=6 * 1024 * 1024),
    )(meta, meta_y, *stores[9:], first)
    query, weight, partial = pl.pallas_call(
        project_kernel,
        out_shape=[
            jax.ShapeDtypeStruct((2, ctx_count, 2, part, DH), jnp.bfloat16),
            jax.ShapeDtypeStruct((late, 2 * DH), jnp.bfloat16),
            jax.ShapeDtypeStruct((2 * images * lat, 2 * DH), jnp.float32),
        ],
        in_specs=[vmem] * 2,
        out_specs=[vmem] * 3,
        scratch_shapes=[pltpu.VMEM((depth, 2 * DH), jnp.bfloat16)],
        cost_estimate=pl.CostEstimate(flops=2 * 10**8, bytes_accessed=16_000_000, transcendentals=0),
        compiler_params=pltpu.CompilerParams(vmem_limit_bytes=8 * 1024 * 1024),
    )(got, kept)
    gated = pl.pallas_call(
        attend_kernel,
        out_shape=jax.ShapeDtypeStruct((ctx_count * 4, part, DH), jnp.bfloat16),
        in_specs=[smem] * 2 + [vmem] * 5,
        out_specs=vmem,
        cost_estimate=pl.CostEstimate(flops=20_000_000_000, bytes_accessed=4 * 1024 * 1024, transcendentals=0),
        compiler_params=pltpu.CompilerParams(vmem_limit_bytes=16 * 1024 * 1024),
    )(meta, meta_y, gate, query, weight, partial, last_columns)
    every = ("groups", "ctx", "head")
    back = lax.all_to_all(gated, every, split_axis=0, concat_axis=0, tiled=True)
    return pl.pallas_call(
        merge_kernel,
        out_shape=jax.ShapeDtypeStruct((part, 2 * width), jnp.bfloat16),
        in_specs=[vmem],
        out_specs=vmem,
        compiler_params=pltpu.CompilerParams(vmem_limit_bytes=4 * 1024 * 1024),
    )(back)


def by_tokens(queries, latents, image_span, image_owner, kv_weight, attn_gate):
    ctx_count = lax.axis_size("ctx")
    rows = lax.all_to_all(queries, "head", split_axis=1, concat_axis=0, tiled=True)
    tok = rows.shape[0]
    width = rows.shape[1]
    lat = latents.shape[1]
    images = image_span.shape[0]
    query_norm = head_norm(rows.astype(jnp.float32), DH).astype(jnp.bfloat16)
    starts = image_span[:, 0]
    ends = image_span[:, 1]
    block_low = jnp.arange(ctx_count, dtype=jnp.int32) * tok
    meets = (starts[None, :] < (block_low + tok)[:, None]) & (ends[None, :] > block_low[:, None])
    counts = jnp.sum(meets.astype(jnp.int32), 1)
    firsts = jnp.sum((ends[None, :] <= block_low[:, None]).astype(jnp.int32), 1)
    slot_iota = jnp.arange(MAXIMG, dtype=jnp.int32)
    wanted = jnp.minimum(firsts[:, None] + slot_iota[None, :], images - 1)
    live = slot_iota[None, :] < counts[:, None]
    holders = image_owner[wanted]
    pieces = lax.all_to_all(latents, "ctx", split_axis=2, concat_axis=0, tiled=True)
    outgoing = jnp.where(live[:, :, None, None], pieces[holders], jnp.zeros((), jnp.bfloat16))
    panels = lax.all_to_all(outgoing, "ctx", split_axis=0, concat_axis=3, tiled=True)
    gathered = lax.all_gather(kv_weight, "ctx", axis=0, tiled=True)
    flat_weight = gathered.reshape(gathered.shape[0], 2 * width)
    both = jnp.dot(
        panels.reshape(MAXIMG * lat, panels.shape[3]),
        flat_weight,
        preferred_element_type=jnp.float32,
    )
    keys_out = head_norm(both[:, :width], DH).astype(jnp.bfloat16)
    values_out = both[:, width:].astype(jnp.bfloat16)
    mine = lax.axis_index("ctx")
    positions = mine * tok + jnp.arange(tok, dtype=jnp.int32)
    inside = (positions[:, None] >= starts[None, :]) & (positions[:, None] < ends[None, :])
    has_image = jnp.any(inside, 1)
    which = jnp.sum(jnp.where(inside, jnp.arange(images, dtype=jnp.int32)[None, :], 0), 1)
    my_first = jnp.sum((ends <= mine * tok).astype(jnp.int32))
    slot = which - my_first
    heads_here = width // DH
    query_heads = query_norm.reshape(tok, heads_here, DH)
    key_heads = keys_out.reshape(MAXIMG * lat, heads_here, DH)
    value_heads = values_out.reshape(MAXIMG * lat, heads_here, DH)
    scores = jnp.einsum(
        "thd,khd->thk", query_heads, key_heads, preferred_element_type=jnp.float32
    ) * DH ** (-0.5)
    owner_slot = jnp.arange(MAXIMG * lat, dtype=jnp.int32) // lat
    selected = (has_image[:, None] & (owner_slot[None, :] == slot[:, None])).astype(jnp.float32)
    weighted = jnp.exp(scores) * selected[:, None, :]
    total = (
        jnp.sum(weighted, -1, keepdims=True) + (1.0 - has_image.astype(jnp.float32))[:, None, None]
    )
    probs = (weighted / total).astype(jnp.bfloat16)
    attended = jnp.einsum("thk,khd->thd", probs, value_heads, preferred_element_type=jnp.float32)
    attended = attended.reshape(tok, width)
    gated = (jnp.tanh(attn_gate)[None, :] * attended).astype(jnp.bfloat16)
    return lax.all_to_all(gated, "head", split_axis=0, concat_axis=1, tiled=True)


def shards(*args):
    ctx_count = lax.axis_size("ctx")
    weight = args[4]
    pairs = lax.axis_size("groups") == 2 and lax.axis_size("head") == 2
    whole_heads = weight.shape[2] == 2 * ctx_count * DH
    whole_blocks = ctx_count == 8 and args[1].shape[2] % (2 * DH) == 0 and args[1].shape[2] > 6 * DH and weight.shape[0] % 32 == 0
    if pairs and whole_heads and whole_blocks and ctx_count & (ctx_count - 1) == 0:
        return by_heads(*args)
    return by_tokens(*args)


def solution(mesh):
    placed = (
        P(("groups", "ctx", "head"), None),
        P(("groups", "ctx"), None, None),
        P("groups", None),
        P("groups"),
        P("ctx", None, "head"),
        P("head"),
    )
    return jax.shard_map(
        shards,
        mesh=mesh,
        in_specs=placed,
        out_specs=P(("groups", "ctx", "head"), None),
        check_vma=False,
    )
```

```python
import jax
import jax.numpy as jnp
from jax import lax
from jax.experimental import pallas as pl
from jax.experimental.pallas import tpu as pltpu
from jax.sharding import PartitionSpec as P

DH = 128
MAXIMG = 4


def head_norm(x, size):
    shaped = x.reshape(x.shape[:-1] + (x.shape[-1] // size, size))
    mean = jnp.mean(shaped, -1, keepdims=True)
    centered = shaped - mean
    spread = jnp.mean(centered * centered, -1, keepdims=True)
    return (centered * lax.rsqrt(spread + 1e-05)).reshape(x.shape)


def row_norm(x):
    centered = x - jnp.mean(x, -1, keepdims=True)
    spread = jnp.mean(centered * centered, -1, keepdims=True)
    return centered * lax.rsqrt(spread + 1e-05)


def place_images(meta_ref, meta_y_ref, near, last, far, last_x, near_y, last_y, far_y, third, fourth, put):
    images = meta_ref.shape[1]
    lat = near.shape[1]
    place = lax.axis_index("ctx")

    def pick(few, one, slot):
        return jnp.where(slot < 3, few[jnp.minimum(slot, 2)], one[0])

    for r, meta in enumerate((meta_ref, meta_y_ref)):
        for i in range(images):
            turn = meta[2, i] ^ place
            slot = turn // 2
            if r == 0:
                one, other = pick(near, last, slot), pick(far, last_x, slot)
            else:
                one = pick(near_y, last_y, slot)
                other = jnp.where(slot == 2, third[0], fourth[0])
                other = jnp.where(slot < 2, far_y[jnp.minimum(slot, 1)], other)
            to = slice((r * images + i) * lat, (r * images + i + 1) * lat)
            put(to, jnp.where(turn % 2 == 0, one, other))


def own_kernel(meta_ref, meta_y_ref, *rest):
    *stores, first_ref, late_ref = rest
    cut = first_ref.shape[1]

    def put(to, image):
        first_ref[to, :] = image[:, :cut]
        late_ref[to, :] = image[:, cut:]

    place_images(meta_ref, meta_y_ref, *stores, put)


def kept_kernel(meta_ref, meta_y_ref, *rest):
    *stores, first_ref, kept_ref = rest
    half = stores[0].shape[2]

    def put(to, image):
        kept_ref[to, :half] = image

    place_images(meta_ref, meta_y_ref, *stores, put)
    kept_ref[:, half:] = first_ref[...]


def project_kernel(got_ref, kept_ref, query_ref, weight_ref, partial_ref, weight):
    ctx_count, _, part, _ = query_ref.shape[1:]
    half = weight.shape[0] // 2
    rows = half // (ctx_count // 2)
    piece = rows // 2
    group = lax.axis_index("groups")
    core = lax.axis_index("head")
    for k in range(2):
        first = (core ^ 1 ^ k) * (ctx_count // 2)
        for s in range(ctx_count // 2):
            for g in range(2):
                at = k * half + s * rows + g * piece
                for n in range(2):
                    weight[at : at + piece, n * DH : (n + 1) * DH] = got_ref[
                        g * ctx_count + first + s, n * piece : (n + 1) * piece, :
                    ]
    cut = kept_ref.shape[1]
    partial_ref[...] = jnp.dot(kept_ref[...], weight[:cut, :], preferred_element_type=jnp.float32)
    weight_ref[...] = weight[cut:, :]
    for r in range(2):
        query = got_ref[pl.ds((group ^ r) * ctx_count, ctx_count), rows : rows + 2 * part, :]
        query = query.reshape(ctx_count * 2 * part, DH).astype(jnp.float32)
        query_ref[r] = row_norm(query).astype(jnp.bfloat16).reshape(query_ref.shape[1:])


def attend_kernel(meta_ref, meta_y_ref, gate_ref, query_ref, weight_ref, partial_ref, late_ref, out_ref):
    ctx_count, _, part, _ = query_ref.shape[1:]
    images = meta_ref.shape[1]
    size = late_ref.shape[0] // 2
    lat = size // images
    count = ctx_count * 2 * part
    group = lax.axis_index("groups")
    core = lax.axis_index("head")
    metas = (meta_ref, meta_y_ref)
    queries = [query_ref[r].reshape(count, DH) for r in range(2)]
    gate = jnp.tanh(gate_ref[pl.ds(group * ctx_count + lax.axis_index("ctx"), 1), :])
    row = lax.broadcasted_iota(jnp.int32, (1, count), 1)
    block = row // part
    position = (block // 2 * 2 + (block % 2 ^ core)) * part + row % part

    def project(r):
        at = slice(r * size, (r + 1) * size)
        both = jnp.dot(late_ref[at, :], weight_ref[...], preferred_element_type=jnp.float32)
        both += partial_ref[at, :]
        return row_norm(both[:, :DH]).astype(jnp.bfloat16), both[:, DH:].astype(jnp.bfloat16)

    def score(r, keys):
        return lax.dot_general(
            keys, queries[r], (((1,), (1,)), ((), ())), preferred_element_type=jnp.float32
        ) * DH ** (-0.5)

    def finish(r, scores, values):
        weighted = []
        for i in range(images):
            inside = (position >= metas[r][0, i]) & (position < metas[r][1, i])
            weighted.append(jnp.where(inside, jnp.exp(scores[i * lat : (i + 1) * lat]), 0.0))
        total = sum(jnp.sum(w, 0, keepdims=True) for w in weighted)
        scale = 1.0 / jnp.where(total > 0.0, total, 1.0)
        probs = jnp.concatenate([(w * scale).astype(jnp.bfloat16) for w in weighted], 0)
        attended = lax.dot_general(
            values, probs, (((0,), (0,)), ((), ())), preferred_element_type=jnp.float32
        ).T
        gated = (gate * attended).astype(jnp.bfloat16).reshape(ctx_count, 2, part, DH)
        for c in range(ctx_count):
            for d in range(2):
                out_ref[((group ^ r) * ctx_count + c) * 2 + (core ^ d)] = gated[c, d]

    projected = [project(r) for r in range(2)]
    scores = [score(r, projected[r][0]) for r in range(2)]
    for r in range(2):
        finish(r, scores[r], projected[r][1])


def split_kernel(query_ref, own_ref, core_ref):
    core = lax.axis_index("head")
    count = own_ref.shape[0]
    for k, to in enumerate((own_ref, core_ref)):
        for c in range(count):
            to[c] = query_ref[:, pl.ds(pl.multiple_of(((core ^ k) * count + c) * DH, DH), DH)]


def join_kernel(weight_ref, *rest):
    *pieces, out_ref = rest
    rows = weight_ref.shape[1]
    part = pieces[0].shape[1]
    out_ref[:, :rows, :] = weight_ref[...]
    for k, piece in enumerate(pieces):
        out_ref[:, rows + k * part : rows + (k + 1) * part, :] = piece[...]


def merge_kernel(back_ref, out_ref):
    count = back_ref.shape[0] // 4
    for n in range(4 * count):
        g, c, h = n // (2 * count), n // 2 % count, n % 2
        at = ((h * 2 + g) * count + c) * DH
        out_ref[:, at : at + DH] = back_ref[n]


def by_heads(queries, latents, image_span, image_owner, kv_weight, attn_gate):
    ctx_count = lax.axis_size("ctx")
    group = lax.axis_index("groups")
    place = lax.axis_index("ctx")
    core = lax.axis_index("head")
    part = queries.shape[0]
    width = kv_weight.shape[2]
    span = width // 2
    rows = kv_weight.shape[0]
    lat, depth = latents.shape[1:]
    images = image_span.shape[0]
    swap = [(0, 1), (1, 0)]
    smem = pl.BlockSpec(memory_space=pltpu.SMEM)
    vmem = pl.BlockSpec(memory_space=pltpu.VMEM)

    def across(x, turn):
        return lax.ppermute(x, "ctx", [(i, i ^ turn) for i in range(ctx_count)])

    share = lax.dynamic_slice_in_dim(latents[0], core * (depth // 2), depth // 2, 1)
    share, meta = lax.optimization_barrier((share, (image_span.T, image_owner[None, :])))
    meta = jnp.concatenate(meta, 0)
    held = [share, across(share, 2), across(share, 4)]
    piece = jax.ShapeDtypeStruct((2 * ctx_count, part, DH), jnp.bfloat16)
    own, sent = pl.pallas_call(
        split_kernel,
        out_shape=[piece] * 2,
        in_specs=[vmem],
        out_specs=[vmem] * 2,
        compiler_params=pltpu.CompilerParams(vmem_limit_bytes=4 * 1024 * 1024),
    )(queries)
    came = lax.ppermute(sent, "head", swap)
    meta_y = lax.ppermute(meta, "groups", swap)
    half = rows // 2
    weight = lax.dynamic_slice_in_dim(kv_weight, group * half, half, 0)
    weight = weight.reshape(half, 2, 2 * ctx_count, DH).transpose(2, 1, 0, 3)
    weight = weight.reshape(2 * ctx_count, 2 * half, DH)
    outgoing = pl.pallas_call(
        join_kernel,
        out_shape=jax.ShapeDtypeStruct((2 * ctx_count, 2 * half + 2 * part, DH), jnp.bfloat16),
        in_specs=[vmem] * 3,
        out_specs=vmem,
        compiler_params=pltpu.CompilerParams(vmem_limit_bytes=6 * 1024 * 1024),
    )(weight, own, came)
    outgoing, meta_y, *held = lax.optimization_barrier((outgoing, meta_y, *held))
    got = lax.all_to_all(outgoing, ("groups", "ctx"), split_axis=0, concat_axis=0, tiled=True)
    near = jnp.stack(held)
    near_y, far, last = lax.optimization_barrier(
        (lax.ppermute(near, "groups", swap), across(near, 1), across(held[2], 2))
    )
    last = last[None]
    last_y = lax.ppermute(last, "groups", swap)
    last_x = across(last, 1)
    far_y = [across(near_y[:2], 1), lax.ppermute(far[2:], "groups", swap), lax.ppermute(last_x, "groups", swap)]
    stores = [near, last, far, last_x, near_y, last_y] + far_y
    stores += [lax.ppermute(x, "head", swap) for x in stores]
    gate = attn_gate.reshape(-1, DH)
    late = 3 * DH
    size = 2 * images * lat
    first, last_columns = pl.pallas_call(
        own_kernel,
        out_shape=[
            jax.ShapeDtypeStruct((size, depth // 2 - late), jnp.bfloat16),
            jax.ShapeDtypeStruct((size, late), jnp.bfloat16),
        ],
        in_specs=[smem] * 2 + [vmem] * 9,
        out_specs=[vmem] * 2,
        cost_estimate=pl.CostEstimate(flops=8_050_000_000, bytes_accessed=2 * 1024 * 1024, transcendentals=0),
        compiler_params=pltpu.CompilerParams(vmem_limit_bytes=6 * 1024 * 1024),
    )(meta, meta_y, *stores[:9])
    kept = pl.pallas_call(
        kept_kernel,
        out_shape=jax.ShapeDtypeStruct((size, depth - late), jnp.bfloat16),
        in_specs=[smem] * 2 + [vmem] * 10,
        out_specs=vmem,
        cost_estimate=pl.CostEstimate(flops=8_050_000_000, bytes_accessed=2 * 1024 * 1024, transcendentals=0),
        compiler_params=pltpu.CompilerParams(vmem_limit_bytes=6 * 1024 * 1024),
    )(meta, meta_y, *stores[9:], first)
    query, weight, partial = pl.pallas_call(
        project_kernel,
        out_shape=[
            jax.ShapeDtypeStruct((2, ctx_count, 2, part, DH), jnp.bfloat16),
            jax.ShapeDtypeStruct((late, 2 * DH), jnp.bfloat16),
            jax.ShapeDtypeStruct((2 * images * lat, 2 * DH), jnp.float32),
        ],
        in_specs=[vmem] * 2,
        out_specs=[vmem] * 3,
        scratch_shapes=[pltpu.VMEM((depth, 2 * DH), jnp.bfloat16)],
        cost_estimate=pl.CostEstimate(flops=2 * 10**8, bytes_accessed=16_000_000, transcendentals=0),
        compiler_params=pltpu.CompilerParams(vmem_limit_bytes=8 * 1024 * 1024),
    )(got, kept)
    gated = pl.pallas_call(
        attend_kernel,
        out_shape=jax.ShapeDtypeStruct((ctx_count * 4, part, DH), jnp.bfloat16),
        in_specs=[smem] * 2 + [vmem] * 5,
        out_specs=vmem,
        cost_estimate=pl.CostEstimate(flops=20_000_000_000, bytes_accessed=4 * 1024 * 1024, transcendentals=0),
        compiler_params=pltpu.CompilerParams(vmem_limit_bytes=16 * 1024 * 1024),
    )(meta, meta_y, gate, query, weight, partial, last_columns)
    every = ("groups", "ctx", "head")
    back = lax.all_to_all(gated, every, split_axis=0, concat_axis=0, tiled=True)
    return pl.pallas_call(
        merge_kernel,
        out_shape=jax.ShapeDtypeStruct((part, 2 * width), jnp.bfloat16),
        in_specs=[vmem],
        out_specs=vmem,
        compiler_params=pltpu.CompilerParams(vmem_limit_bytes=4 * 1024 * 1024),
    )(back)


def by_tokens(queries, latents, image_span, image_owner, kv_weight, attn_gate):
    ctx_count = lax.axis_size("ctx")
    rows = lax.all_to_all(queries, "head", split_axis=1, concat_axis=0, tiled=True)
    tok = rows.shape[0]
    width = rows.shape[1]
    lat = latents.shape[1]
    images = image_span.shape[0]
    query_norm = head_norm(rows.astype(jnp.float32), DH).astype(jnp.bfloat16)
    starts = image_span[:, 0]
    ends = image_span[:, 1]
    block_low = jnp.arange(ctx_count, dtype=jnp.int32) * tok
    meets = (starts[None, :] < (block_low + tok)[:, None]) & (ends[None, :] > block_low[:, None])
    counts = jnp.sum(meets.astype(jnp.int32), 1)
    firsts = jnp.sum((ends[None, :] <= block_low[:, None]).astype(jnp.int32), 1)
    slot_iota = jnp.arange(MAXIMG, dtype=jnp.int32)
    wanted = jnp.minimum(firsts[:, None] + slot_iota[None, :], images - 1)
    live = slot_iota[None, :] < counts[:, None]
    holders = image_owner[wanted]
    pieces = lax.all_to_all(latents, "ctx", split_axis=2, concat_axis=0, tiled=True)
    outgoing = jnp.where(live[:, :, None, None], pieces[holders], jnp.zeros((), jnp.bfloat16))
    panels = lax.all_to_all(outgoing, "ctx", split_axis=0, concat_axis=3, tiled=True)
    gathered = lax.all_gather(kv_weight, "ctx", axis=0, tiled=True)
    flat_weight = gathered.reshape(gathered.shape[0], 2 * width)
    both = jnp.dot(
        panels.reshape(MAXIMG * lat, panels.shape[3]),
        flat_weight,
        preferred_element_type=jnp.float32,
    )
    keys_out = head_norm(both[:, :width], DH).astype(jnp.bfloat16)
    values_out = both[:, width:].astype(jnp.bfloat16)
    mine = lax.axis_index("ctx")
    positions = mine * tok + jnp.arange(tok, dtype=jnp.int32)
    inside = (positions[:, None] >= starts[None, :]) & (positions[:, None] < ends[None, :])
    has_image = jnp.any(inside, 1)
    which = jnp.sum(jnp.where(inside, jnp.arange(images, dtype=jnp.int32)[None, :], 0), 1)
    my_first = jnp.sum((ends <= mine * tok).astype(jnp.int32))
    slot = which - my_first
    heads_here = width // DH
    query_heads = query_norm.reshape(tok, heads_here, DH)
    key_heads = keys_out.reshape(MAXIMG * lat, heads_here, DH)
    value_heads = values_out.reshape(MAXIMG * lat, heads_here, DH)
    scores = jnp.einsum(
        "thd,khd->thk", query_heads, key_heads, preferred_element_type=jnp.float32
    ) * DH ** (-0.5)
    owner_slot = jnp.arange(MAXIMG * lat, dtype=jnp.int32) // lat
    selected = (has_image[:, None] & (owner_slot[None, :] == slot[:, None])).astype(jnp.float32)
    weighted = jnp.exp(scores) * selected[:, None, :]
    total = (
        jnp.sum(weighted, -1, keepdims=True) + (1.0 - has_image.astype(jnp.float32))[:, None, None]
    )
    probs = (weighted / total).astype(jnp.bfloat16)
    attended = jnp.einsum("thk,khd->thd", probs, value_heads, preferred_element_type=jnp.float32)
    attended = attended.reshape(tok, width)
    gated = (jnp.tanh(attn_gate)[None, :] * attended).astype(jnp.bfloat16)
    return lax.all_to_all(gated, "head", split_axis=0, concat_axis=1, tiled=True)


def shards(*args):
    ctx_count = lax.axis_size("ctx")
    weight = args[4]
    pairs = lax.axis_size("groups") == 2 and lax.axis_size("head") == 2
    whole_heads = weight.shape[2] == 2 * ctx_count * DH
    whole_blocks = ctx_count == 8 and args[1].shape[2] % (2 * DH) == 0 and args[1].shape[2] > 6 * DH and weight.shape[0] % 32 == 0
    if pairs and whole_heads and whole_blocks and ctx_count & (ctx_count - 1) == 0:
        return by_heads(*args)
    return by_tokens(*args)


def solution(mesh):
    placed = (
        P(("groups", "ctx", "head"), None),
        P(("groups", "ctx"), None, None),
        P("groups", None),
        P("groups"),
        P("ctx", None, "head"),
        P("head"),
    )
    return jax.shard_map(
        shards,
        mesh=mesh,
        in_specs=placed,
        out_specs=P(("groups", "ctx", "head"), None),
        check_vma=False,
    )
```

```python
import jax
import jax.numpy as jnp
from jax import lax
from jax.experimental import pallas as pl
from jax.experimental.pallas import tpu as pltpu
from jax.sharding import PartitionSpec as P

DH = 128
MAXIMG = 4


def head_norm(x, size):
    shaped = x.reshape(x.shape[:-1] + (x.shape[-1] // size, size))
    mean = jnp.mean(shaped, -1, keepdims=True)
    centered = shaped - mean
    spread = jnp.mean(centered * centered, -1, keepdims=True)
    return (centered * lax.rsqrt(spread + 1e-05)).reshape(x.shape)


def row_norm(x):
    centered = x - jnp.mean(x, -1, keepdims=True)
    spread = jnp.mean(centered * centered, -1, keepdims=True)
    return centered * lax.rsqrt(spread + 1e-05)


def place_images(meta_ref, meta_y_ref, near, last, far, last_x, near_y, last_y, far_y, third, fourth, put):
    images = meta_ref.shape[1]
    lat = near.shape[1]
    place = lax.axis_index("ctx")

    def pick(few, one, slot):
        return jnp.where(slot < 3, few[jnp.minimum(slot, 2)], one[0])

    for r, meta in enumerate((meta_ref, meta_y_ref)):
        for i in range(images):
            turn = meta[2, i] ^ place
            slot = turn // 2
            if r == 0:
                one, other = pick(near, last, slot), pick(far, last_x, slot)
            else:
                one = pick(near_y, last_y, slot)
                other = jnp.where(slot == 2, third[0], fourth[0])
                other = jnp.where(slot < 2, far_y[jnp.minimum(slot, 1)], other)
            to = slice((r * images + i) * lat, (r * images + i + 1) * lat)
            put(to, jnp.where(turn % 2 == 0, one, other))


def own_kernel(meta_ref, meta_y_ref, *rest):
    *stores, first_ref, late_ref = rest
    cut = first_ref.shape[1]

    def put(to, image):
        first_ref[to, :] = image[:, :cut]
        late_ref[to, :] = image[:, cut:]

    place_images(meta_ref, meta_y_ref, *stores, put)


def kept_kernel(meta_ref, meta_y_ref, *rest):
    *stores, first_ref, kept_ref = rest
    half = stores[0].shape[2]

    def put(to, image):
        kept_ref[to, :half] = image

    place_images(meta_ref, meta_y_ref, *stores, put)
    kept_ref[:, half:] = first_ref[...]


def project_kernel(got_ref, kept_ref, query_ref, weight_ref, partial_ref, weight):
    ctx_count, _, part, _ = query_ref.shape[1:]
    half = weight.shape[0] // 2
    rows = half // (ctx_count // 2)
    piece = rows // 2
    group = lax.axis_index("groups")
    core = lax.axis_index("head")
    for k in range(2):
        first = (core ^ 1 ^ k) * (ctx_count // 2)
        for s in range(ctx_count // 2):
            for g in range(2):
                at = k * half + s * rows + g * piece
                for n in range(2):
                    weight[at : at + piece, n * DH : (n + 1) * DH] = got_ref[
                        g * ctx_count + first + s, n * piece : (n + 1) * piece, :
                    ]
    cut = kept_ref.shape[1]
    partial_ref[...] = jnp.dot(kept_ref[...], weight[:cut, :], preferred_element_type=jnp.float32)
    weight_ref[...] = weight[cut:, :]
    for r in range(2):
        query = got_ref[pl.ds((group ^ r) * ctx_count, ctx_count), rows : rows + 2 * part, :]
        query = query.reshape(ctx_count * 2 * part, DH).astype(jnp.float32)
        query_ref[r] = row_norm(query).astype(jnp.bfloat16).reshape(query_ref.shape[1:])


def attend_kernel(meta_ref, meta_y_ref, gate_ref, query_ref, weight_ref, partial_ref, late_ref, out_ref):
    ctx_count, _, part, _ = query_ref.shape[1:]
    images = meta_ref.shape[1]
    size = late_ref.shape[0] // 2
    lat = size // images
    count = ctx_count * 2 * part
    group = lax.axis_index("groups")
    core = lax.axis_index("head")
    metas = (meta_ref, meta_y_ref)
    queries = [query_ref[r].reshape(count, DH) for r in range(2)]
    gate = jnp.tanh(gate_ref[pl.ds(group * ctx_count + lax.axis_index("ctx"), 1), :])
    row = lax.broadcasted_iota(jnp.int32, (1, count), 1)
    block = row // part
    position = (block // 2 * 2 + (block % 2 ^ core)) * part + row % part

    def project(r):
        at = slice(r * size, (r + 1) * size)
        both = jnp.dot(late_ref[at, :], weight_ref[...], preferred_element_type=jnp.float32)
        both += partial_ref[at, :]
        return row_norm(both[:, :DH]).astype(jnp.bfloat16), both[:, DH:].astype(jnp.bfloat16)

    def score(r, keys):
        return lax.dot_general(
            keys, queries[r], (((1,), (1,)), ((), ())), preferred_element_type=jnp.float32
        ) * DH ** (-0.5)

    def finish(r, scores, values):
        weighted = []
        for i in range(images):
            inside = (position >= metas[r][0, i]) & (position < metas[r][1, i])
            weighted.append(jnp.where(inside, jnp.exp(scores[i * lat : (i + 1) * lat]), 0.0))
        total = sum(jnp.sum(w, 0, keepdims=True) for w in weighted)
        scale = 1.0 / jnp.where(total > 0.0, total, 1.0)
        probs = jnp.concatenate([w.astype(jnp.bfloat16) for w in weighted], 0)
        attended = lax.dot_general(
            values, probs, (((0,), (0,)), ((), ())), preferred_element_type=jnp.float32
        )
        attended = (attended * scale).T
        gated = (gate * attended).astype(jnp.bfloat16).reshape(ctx_count, 2, part, DH)
        for c in range(ctx_count):
            for d in range(2):
                out_ref[((group ^ r) * ctx_count + c) * 2 + (core ^ d)] = gated[c, d]

    projected = [project(r) for r in range(2)]
    scores = [score(r, projected[r][0]) for r in range(2)]
    for r in range(2):
        finish(r, scores[r], projected[r][1])


def split_kernel(query_ref, own_ref, core_ref):
    core = lax.axis_index("head")
    count = own_ref.shape[0]
    for k, to in enumerate((own_ref, core_ref)):
        for c in range(count):
            to[c] = query_ref[:, pl.ds(pl.multiple_of(((core ^ k) * count + c) * DH, DH), DH)]


def join_kernel(weight_ref, *rest):
    *pieces, out_ref = rest
    rows = weight_ref.shape[1]
    part = pieces[0].shape[1]
    out_ref[:, :rows, :] = weight_ref[...]
    for k, piece in enumerate(pieces):
        out_ref[:, rows + k * part : rows + (k + 1) * part, :] = piece[...]


def merge_kernel(back_ref, out_ref):
    count = back_ref.shape[0] // 4
    for n in range(4 * count):
        g, c, h = n // (2 * count), n // 2 % count, n % 2
        at = ((h * 2 + g) * count + c) * DH
        out_ref[:, at : at + DH] = back_ref[n]


def by_heads(queries, latents, image_span, image_owner, kv_weight, attn_gate):
    ctx_count = lax.axis_size("ctx")
    group = lax.axis_index("groups")
    place = lax.axis_index("ctx")
    core = lax.axis_index("head")
    part = queries.shape[0]
    width = kv_weight.shape[2]
    span = width // 2
    rows = kv_weight.shape[0]
    lat, depth = latents.shape[1:]
    images = image_span.shape[0]
    swap = [(0, 1), (1, 0)]
    smem = pl.BlockSpec(memory_space=pltpu.SMEM)
    vmem = pl.BlockSpec(memory_space=pltpu.VMEM)

    def across(x, turn):
        return lax.ppermute(x, "ctx", [(i, i ^ turn) for i in range(ctx_count)])

    share = lax.dynamic_slice_in_dim(latents[0], core * (depth // 2), depth // 2, 1)
    share, meta = lax.optimization_barrier((share, (image_span.T, image_owner[None, :])))
    meta = jnp.concatenate(meta, 0)
    held = [share, across(share, 2), across(share, 4)]
    piece = jax.ShapeDtypeStruct((2 * ctx_count, part, DH), jnp.bfloat16)
    own, sent = pl.pallas_call(
        split_kernel,
        out_shape=[piece] * 2,
        in_specs=[vmem],
        out_specs=[vmem] * 2,
        compiler_params=pltpu.CompilerParams(vmem_limit_bytes=4 * 1024 * 1024),
    )(queries)
    came = lax.ppermute(sent, "head", swap)
    meta_y = lax.ppermute(meta, "groups", swap)
    half = rows // 2
    weight = lax.dynamic_slice_in_dim(kv_weight, group * half, half, 0)
    weight = weight.reshape(half, 2, 2 * ctx_count, DH).transpose(2, 1, 0, 3)
    weight = weight.reshape(2 * ctx_count, 2 * half, DH)
    outgoing = pl.pallas_call(
        join_kernel,
        out_shape=jax.ShapeDtypeStruct((2 * ctx_count, 2 * half + 2 * part, DH), jnp.bfloat16),
        in_specs=[vmem] * 3,
        out_specs=vmem,
        compiler_params=pltpu.CompilerParams(vmem_limit_bytes=6 * 1024 * 1024),
    )(weight, own, came)
    outgoing, meta_y, *held = lax.optimization_barrier((outgoing, meta_y, *held))
    got = lax.all_to_all(outgoing, ("groups", "ctx"), split_axis=0, concat_axis=0, tiled=True)
    near = jnp.stack(held)
    near_y, far, last = lax.optimization_barrier(
        (lax.ppermute(near, "groups", swap), across(near, 1), across(held[2], 2))
    )
    last = last[None]
    last_y = lax.ppermute(last, "groups", swap)
    last_x = across(last, 1)
    far_y = [across(near_y[:2], 1), lax.ppermute(far[2:], "groups", swap), lax.ppermute(last_x, "groups", swap)]
    stores = [near, last, far, last_x, near_y, last_y] + far_y
    stores += [lax.ppermute(x, "head", swap) for x in stores]
    gate = attn_gate.reshape(-1, DH)
    late = 3 * DH
    size = 2 * images * lat
    first, last_columns = pl.pallas_call(
        own_kernel,
        out_shape=[
            jax.ShapeDtypeStruct((size, depth // 2 - late), jnp.bfloat16),
            jax.ShapeDtypeStruct((size, late), jnp.bfloat16),
        ],
        in_specs=[smem] * 2 + [vmem] * 9,
        out_specs=[vmem] * 2,
        cost_estimate=pl.CostEstimate(flops=8_050_000_000, bytes_accessed=2 * 1024 * 1024, transcendentals=0),
        compiler_params=pltpu.CompilerParams(vmem_limit_bytes=6 * 1024 * 1024),
    )(meta, meta_y, *stores[:9])
    kept = pl.pallas_call(
        kept_kernel,
        out_shape=jax.ShapeDtypeStruct((size, depth - late), jnp.bfloat16),
        in_specs=[smem] * 2 + [vmem] * 10,
        out_specs=vmem,
        cost_estimate=pl.CostEstimate(flops=8_050_000_000, bytes_accessed=2 * 1024 * 1024, transcendentals=0),
        compiler_params=pltpu.CompilerParams(vmem_limit_bytes=6 * 1024 * 1024),
    )(meta, meta_y, *stores[9:], first)
    query, weight, partial = pl.pallas_call(
        project_kernel,
        out_shape=[
            jax.ShapeDtypeStruct((2, ctx_count, 2, part, DH), jnp.bfloat16),
            jax.ShapeDtypeStruct((late, 2 * DH), jnp.bfloat16),
            jax.ShapeDtypeStruct((2 * images * lat, 2 * DH), jnp.float32),
        ],
        in_specs=[vmem] * 2,
        out_specs=[vmem] * 3,
        scratch_shapes=[pltpu.VMEM((depth, 2 * DH), jnp.bfloat16)],
        cost_estimate=pl.CostEstimate(flops=2 * 10**8, bytes_accessed=16_000_000, transcendentals=0),
        compiler_params=pltpu.CompilerParams(vmem_limit_bytes=8 * 1024 * 1024),
    )(got, kept)
    gated = pl.pallas_call(
        attend_kernel,
        out_shape=jax.ShapeDtypeStruct((ctx_count * 4, part, DH), jnp.bfloat16),
        in_specs=[smem] * 2 + [vmem] * 5,
        out_specs=vmem,
        cost_estimate=pl.CostEstimate(flops=20_000_000_000, bytes_accessed=4 * 1024 * 1024, transcendentals=0),
        compiler_params=pltpu.CompilerParams(vmem_limit_bytes=16 * 1024 * 1024),
    )(meta, meta_y, gate, query, weight, partial, last_columns)
    every = ("groups", "ctx", "head")
    back = lax.all_to_all(gated, every, split_axis=0, concat_axis=0, tiled=True)
    return pl.pallas_call(
        merge_kernel,
        out_shape=jax.ShapeDtypeStruct((part, 2 * width), jnp.bfloat16),
        in_specs=[vmem],
        out_specs=vmem,
        compiler_params=pltpu.CompilerParams(vmem_limit_bytes=4 * 1024 * 1024),
    )(back)


def by_tokens(queries, latents, image_span, image_owner, kv_weight, attn_gate):
    ctx_count = lax.axis_size("ctx")
    rows = lax.all_to_all(queries, "head", split_axis=1, concat_axis=0, tiled=True)
    tok = rows.shape[0]
    width = rows.shape[1]
    lat = latents.shape[1]
    images = image_span.shape[0]
    query_norm = head_norm(rows.astype(jnp.float32), DH).astype(jnp.bfloat16)
    starts = image_span[:, 0]
    ends = image_span[:, 1]
    block_low = jnp.arange(ctx_count, dtype=jnp.int32) * tok
    meets = (starts[None, :] < (block_low + tok)[:, None]) & (ends[None, :] > block_low[:, None])
    counts = jnp.sum(meets.astype(jnp.int32), 1)
    firsts = jnp.sum((ends[None, :] <= block_low[:, None]).astype(jnp.int32), 1)
    slot_iota = jnp.arange(MAXIMG, dtype=jnp.int32)
    wanted = jnp.minimum(firsts[:, None] + slot_iota[None, :], images - 1)
    live = slot_iota[None, :] < counts[:, None]
    holders = image_owner[wanted]
    pieces = lax.all_to_all(latents, "ctx", split_axis=2, concat_axis=0, tiled=True)
    outgoing = jnp.where(live[:, :, None, None], pieces[holders], jnp.zeros((), jnp.bfloat16))
    panels = lax.all_to_all(outgoing, "ctx", split_axis=0, concat_axis=3, tiled=True)
    gathered = lax.all_gather(kv_weight, "ctx", axis=0, tiled=True)
    flat_weight = gathered.reshape(gathered.shape[0], 2 * width)
    both = jnp.dot(
        panels.reshape(MAXIMG * lat, panels.shape[3]),
        flat_weight,
        preferred_element_type=jnp.float32,
    )
    keys_out = head_norm(both[:, :width], DH).astype(jnp.bfloat16)
    values_out = both[:, width:].astype(jnp.bfloat16)
    mine = lax.axis_index("ctx")
    positions = mine * tok + jnp.arange(tok, dtype=jnp.int32)
    inside = (positions[:, None] >= starts[None, :]) & (positions[:, None] < ends[None, :])
    has_image = jnp.any(inside, 1)
    which = jnp.sum(jnp.where(inside, jnp.arange(images, dtype=jnp.int32)[None, :], 0), 1)
    my_first = jnp.sum((ends <= mine * tok).astype(jnp.int32))
    slot = which - my_first
    heads_here = width // DH
    query_heads = query_norm.reshape(tok, heads_here, DH)
    key_heads = keys_out.reshape(MAXIMG * lat, heads_here, DH)
    value_heads = values_out.reshape(MAXIMG * lat, heads_here, DH)
    scores = jnp.einsum(
        "thd,khd->thk", query_heads, key_heads, preferred_element_type=jnp.float32
    ) * DH ** (-0.5)
    owner_slot = jnp.arange(MAXIMG * lat, dtype=jnp.int32) // lat
    selected = (has_image[:, None] & (owner_slot[None, :] == slot[:, None])).astype(jnp.float32)
    weighted = jnp.exp(scores) * selected[:, None, :]
    total = (
        jnp.sum(weighted, -1, keepdims=True) + (1.0 - has_image.astype(jnp.float32))[:, None, None]
    )
    probs = (weighted / total).astype(jnp.bfloat16)
    attended = jnp.einsum("thk,khd->thd", probs, value_heads, preferred_element_type=jnp.float32)
    attended = attended.reshape(tok, width)
    gated = (jnp.tanh(attn_gate)[None, :] * attended).astype(jnp.bfloat16)
    return lax.all_to_all(gated, "head", split_axis=0, concat_axis=1, tiled=True)


def shards(*args):
    ctx_count = lax.axis_size("ctx")
    weight = args[4]
    pairs = lax.axis_size("groups") == 2 and lax.axis_size("head") == 2
    whole_heads = weight.shape[2] == 2 * ctx_count * DH
    whole_blocks = ctx_count == 8 and args[1].shape[2] % (2 * DH) == 0 and args[1].shape[2] > 6 * DH and weight.shape[0] % 32 == 0
    if pairs and whole_heads and whole_blocks and ctx_count & (ctx_count - 1) == 0:
        return by_heads(*args)
    return by_tokens(*args)


def solution(mesh):
    placed = (
        P(("groups", "ctx", "head"), None),
        P(("groups", "ctx"), None, None),
        P("groups", None),
        P("groups"),
        P("ctx", None, "head"),
        P("head"),
    )
    return jax.shard_map(
        shards,
        mesh=mesh,
        in_specs=placed,
        out_specs=P(("groups", "ctx", "head"), None),
        check_vma=False,
    )
```

```python
import jax
import jax.numpy as jnp
from jax import lax
from jax.experimental import pallas as pl
from jax.experimental.pallas import tpu as pltpu
from jax.sharding import PartitionSpec as P

DH = 128
MAXIMG = 4


def head_norm(x, size):
    shaped = x.reshape(x.shape[:-1] + (x.shape[-1] // size, size))
    mean = jnp.mean(shaped, -1, keepdims=True)
    centered = shaped - mean
    spread = jnp.mean(centered * centered, -1, keepdims=True)
    return (centered * lax.rsqrt(spread + 1e-05)).reshape(x.shape)


def row_norm(x):
    centered = x - jnp.mean(x, -1, keepdims=True)
    spread = jnp.mean(centered * centered, -1, keepdims=True)
    return centered * lax.rsqrt(spread + 1e-05)


def place_images(meta_ref, meta_y_ref, near, last, far, last_x, near_y, last_y, far_y, third, fourth, put):
    images = meta_ref.shape[1]
    lat = near.shape[1]
    place = lax.axis_index("ctx")

    def pick(few, one, slot):
        return jnp.where(slot < 3, few[jnp.minimum(slot, 2)], one[0])

    for r, meta in enumerate((meta_ref, meta_y_ref)):
        for i in range(images):
            turn = meta[2, i] ^ place
            slot = turn // 2
            if r == 0:
                one, other = pick(near, last, slot), pick(far, last_x, slot)
            else:
                one = pick(near_y, last_y, slot)
                other = jnp.where(slot == 2, third[0], fourth[0])
                other = jnp.where(slot < 2, far_y[jnp.minimum(slot, 1)], other)
            to = slice((r * images + i) * lat, (r * images + i + 1) * lat)
            put(to, jnp.where(turn % 2 == 0, one, other))


def own_kernel(meta_ref, meta_y_ref, *rest):
    *stores, first_ref, late_ref = rest
    cut = first_ref.shape[1]

    def put(to, image):
        first_ref[to, :] = image[:, :cut]
        late_ref[to, :] = image[:, cut:]

    place_images(meta_ref, meta_y_ref, *stores, put)


def kept_kernel(meta_ref, meta_y_ref, *rest):
    *stores, first_ref, kept_ref = rest
    half = stores[0].shape[2]

    def put(to, image):
        kept_ref[to, :half] = image

    place_images(meta_ref, meta_y_ref, *stores, put)
    kept_ref[:, half:] = first_ref[...]


def project_kernel(got_ref, kept_ref, query_ref, weight_ref, partial_ref, weight):
    ctx_count, _, part, _ = query_ref.shape[1:]
    half = weight.shape[0] // 2
    rows = half // (ctx_count // 2)
    piece = rows // 2
    group = lax.axis_index("groups")
    core = lax.axis_index("head")
    for k in range(2):
        first = (core ^ 1 ^ k) * (ctx_count // 2)
        for s in range(ctx_count // 2):
            for g in range(2):
                at = k * half + s * rows + g * piece
                for n in range(2):
                    weight[at : at + piece, n * DH : (n + 1) * DH] = got_ref[
                        g * ctx_count + first + s, n * piece : (n + 1) * piece, :
                    ]
    cut = kept_ref.shape[1]
    partial_ref[...] = jnp.dot(kept_ref[...], weight[:cut, :], preferred_element_type=jnp.float32)
    weight_ref[...] = weight[cut:, :]
    for r in range(2):
        query = got_ref[pl.ds((group ^ r) * ctx_count, ctx_count), rows : rows + 2 * part, :]
        query = query.reshape(ctx_count * 2 * part, DH).astype(jnp.float32)
        query_ref[r] = row_norm(query).astype(jnp.bfloat16).reshape(query_ref.shape[1:])


def attend_kernel(meta_ref, meta_y_ref, gate_ref, query_ref, weight_ref, partial_ref, late_ref, out_ref):
    ctx_count, _, part, _ = query_ref.shape[1:]
    images = meta_ref.shape[1]
    size = late_ref.shape[0] // 2
    lat = size // images
    count = ctx_count * 2 * part
    group = lax.axis_index("groups")
    core = lax.axis_index("head")
    metas = (meta_ref, meta_y_ref)
    queries = [query_ref[r].reshape(count, DH) for r in range(2)]
    gate = jnp.tanh(gate_ref[pl.ds(group * ctx_count + lax.axis_index("ctx"), 1), :])
    row = lax.broadcasted_iota(jnp.int32, (1, count), 1)
    block = row // part
    position = (block // 2 * 2 + (block % 2 ^ core)) * part + row % part

    def project(r):
        at = slice(r * size, (r + 1) * size)
        both = jnp.dot(late_ref[at, :], weight_ref[...], preferred_element_type=jnp.float32)
        both += partial_ref[at, :]
        return row_norm(both[:, :DH]).astype(jnp.bfloat16), both[:, DH:].astype(jnp.bfloat16)

    def score(r, keys):
        return lax.dot_general(
            keys, queries[r], (((1,), (1,)), ((), ())), preferred_element_type=jnp.float32
        ) * DH ** (-0.5)

    def finish(r, scores, values):
        weighted = []
        for i in range(images):
            inside = (position >= metas[r][0, i]) & (position < metas[r][1, i])
            weighted.append(jnp.where(inside, jnp.exp(scores[i * lat : (i + 1) * lat]), 0.0))
        total = sum(jnp.sum(w, 0, keepdims=True) for w in weighted)
        scale = 1.0 / jnp.where(total > 0.0, total, 1.0)
        probs = jnp.concatenate([(w * scale).astype(jnp.bfloat16) for w in weighted], 0)
        attended = lax.dot_general(
            values, probs, (((0,), (0,)), ((), ())), preferred_element_type=jnp.float32
        ).T
        gated = (gate * attended).astype(jnp.bfloat16).reshape(ctx_count, 2, part, DH)
        for c in range(ctx_count):
            for d in range(2):
                out_ref[((group ^ r) * ctx_count + c) * 2 + (core ^ d)] = gated[c, d]

    projected = [project(r) for r in range(2)]
    scores = [score(r, projected[r][0]) for r in range(2)]
    for r in range(2):
        finish(r, scores[r], projected[r][1])


def split_kernel(query_ref, own_ref, core_ref):
    core = lax.axis_index("head")
    count = own_ref.shape[0]
    for k, to in enumerate((own_ref, core_ref)):
        for c in range(count):
            to[c] = query_ref[:, pl.ds(pl.multiple_of(((core ^ k) * count + c) * DH, DH), DH)]


def join_kernel(weight_ref, *rest):
    *pieces, out_ref = rest
    rows = weight_ref.shape[1]
    part = pieces[0].shape[1]
    out_ref[:, :rows, :] = weight_ref[...]
    for k, piece in enumerate(pieces):
        out_ref[:, rows + k * part : rows + (k + 1) * part, :] = piece[...]


def merge_kernel(back_ref, out_ref):
    count = back_ref.shape[0] // 4
    for n in range(4 * count):
        g, c, h = n // (2 * count), n // 2 % count, n % 2
        at = ((h * 2 + g) * count + c) * DH
        out_ref[:, at : at + DH] = back_ref[n]


def by_heads(queries, latents, image_span, image_owner, kv_weight, attn_gate):
    ctx_count = lax.axis_size("ctx")
    group = lax.axis_index("groups")
    place = lax.axis_index("ctx")
    core = lax.axis_index("head")
    part = queries.shape[0]
    width = kv_weight.shape[2]
    span = width // 2
    rows = kv_weight.shape[0]
    lat, depth = latents.shape[1:]
    images = image_span.shape[0]
    swap = [(0, 1), (1, 0)]
    smem = pl.BlockSpec(memory_space=pltpu.SMEM)
    vmem = pl.BlockSpec(memory_space=pltpu.VMEM)

    def across(x, turn):
        return lax.ppermute(x, "ctx", [(i, i ^ turn) for i in range(ctx_count)])

    share = lax.dynamic_slice_in_dim(latents[0], core * (depth // 2), depth // 2, 1)
    share, meta = lax.optimization_barrier((share, (image_span.T, image_owner[None, :])))
    meta = jnp.concatenate(meta, 0)
    held = [share, across(share, 2), across(share, 4)]
    piece = jax.ShapeDtypeStruct((2 * ctx_count, part, DH), jnp.bfloat16)
    own, sent = pl.pallas_call(
        split_kernel,
        out_shape=[piece] * 2,
        in_specs=[vmem],
        out_specs=[vmem] * 2,
        compiler_params=pltpu.CompilerParams(vmem_limit_bytes=4 * 1024 * 1024),
    )(queries)
    came = lax.ppermute(sent, "head", swap)
    meta_y = lax.ppermute(meta, "groups", swap)
    half = rows // 2
    weight = lax.dynamic_slice_in_dim(kv_weight, group * half, half, 0)
    weight = weight.reshape(half, 2, 2 * ctx_count, DH).transpose(2, 1, 0, 3)
    weight = weight.reshape(2 * ctx_count, 2 * half, DH)
    outgoing = pl.pallas_call(
        join_kernel,
        out_shape=jax.ShapeDtypeStruct((2 * ctx_count, 2 * half + 2 * part, DH), jnp.bfloat16),
        in_specs=[vmem] * 3,
        out_specs=vmem,
        compiler_params=pltpu.CompilerParams(vmem_limit_bytes=6 * 1024 * 1024),
    )(weight, own, came)
    outgoing, meta_y, *held = lax.optimization_barrier((outgoing, meta_y, *held))
    got = lax.all_to_all(outgoing, ("groups", "ctx"), split_axis=0, concat_axis=0, tiled=True)
    near = jnp.stack(held)
    near_y, far, last = lax.optimization_barrier(
        (lax.ppermute(near, "groups", swap), across(near, 1), across(held[2], 2))
    )
    last = last[None]
    last_y = lax.ppermute(last, "groups", swap)
    last_x = across(last, 1)
    far_y = [across(near_y[:2], 1), lax.ppermute(far[2:], "groups", swap), lax.ppermute(last_x, "groups", swap)]
    stores = [near, last, far, last_x, near_y, last_y] + far_y
    stores += [lax.ppermute(x, "head", swap) for x in stores]
    gate = attn_gate.reshape(-1, DH)
    late = 4 * DH
    size = 2 * images * lat
    first, last_columns = pl.pallas_call(
        own_kernel,
        out_shape=[
            jax.ShapeDtypeStruct((size, depth // 2 - late), jnp.bfloat16),
            jax.ShapeDtypeStruct((size, late), jnp.bfloat16),
        ],
        in_specs=[smem] * 2 + [vmem] * 9,
        out_specs=[vmem] * 2,
        cost_estimate=pl.CostEstimate(flops=8_050_000_000, bytes_accessed=2 * 1024 * 1024, transcendentals=0),
        compiler_params=pltpu.CompilerParams(vmem_limit_bytes=6 * 1024 * 1024),
    )(meta, meta_y, *stores[:9])
    kept = pl.pallas_call(
        kept_kernel,
        out_shape=jax.ShapeDtypeStruct((size, depth - late), jnp.bfloat16),
        in_specs=[smem] * 2 + [vmem] * 10,
        out_specs=vmem,
        cost_estimate=pl.CostEstimate(flops=8_050_000_000, bytes_accessed=2 * 1024 * 1024, transcendentals=0),
        compiler_params=pltpu.CompilerParams(vmem_limit_bytes=6 * 1024 * 1024),
    )(meta, meta_y, *stores[9:], first)
    query, weight, partial = pl.pallas_call(
        project_kernel,
        out_shape=[
            jax.ShapeDtypeStruct((2, ctx_count, 2, part, DH), jnp.bfloat16),
            jax.ShapeDtypeStruct((late, 2 * DH), jnp.bfloat16),
            jax.ShapeDtypeStruct((2 * images * lat, 2 * DH), jnp.float32),
        ],
        in_specs=[vmem] * 2,
        out_specs=[vmem] * 3,
        scratch_shapes=[pltpu.VMEM((depth, 2 * DH), jnp.bfloat16)],
        cost_estimate=pl.CostEstimate(flops=2 * 10**8, bytes_accessed=16_000_000, transcendentals=0),
        compiler_params=pltpu.CompilerParams(vmem_limit_bytes=8 * 1024 * 1024),
    )(got, kept)
    gated = pl.pallas_call(
        attend_kernel,
        out_shape=jax.ShapeDtypeStruct((ctx_count * 4, part, DH), jnp.bfloat16),
        in_specs=[smem] * 2 + [vmem] * 5,
        out_specs=vmem,
        cost_estimate=pl.CostEstimate(flops=20_000_000_000, bytes_accessed=4 * 1024 * 1024, transcendentals=0),
        compiler_params=pltpu.CompilerParams(vmem_limit_bytes=16 * 1024 * 1024),
    )(meta, meta_y, gate, query, weight, partial, last_columns)
    every = ("groups", "ctx", "head")
    back = lax.all_to_all(gated, every, split_axis=0, concat_axis=0, tiled=True)
    return pl.pallas_call(
        merge_kernel,
        out_shape=jax.ShapeDtypeStruct((part, 2 * width), jnp.bfloat16),
        in_specs=[vmem],
        out_specs=vmem,
        compiler_params=pltpu.CompilerParams(vmem_limit_bytes=4 * 1024 * 1024),
    )(back)


def by_tokens(queries, latents, image_span, image_owner, kv_weight, attn_gate):
    ctx_count = lax.axis_size("ctx")
    rows = lax.all_to_all(queries, "head", split_axis=1, concat_axis=0, tiled=True)
    tok = rows.shape[0]
    width = rows.shape[1]
    lat = latents.shape[1]
    images = image_span.shape[0]
    query_norm = head_norm(rows.astype(jnp.float32), DH).astype(jnp.bfloat16)
    starts = image_span[:, 0]
    ends = image_span[:, 1]
    block_low = jnp.arange(ctx_count, dtype=jnp.int32) * tok
    meets = (starts[None, :] < (block_low + tok)[:, None]) & (ends[None, :] > block_low[:, None])
    counts = jnp.sum(meets.astype(jnp.int32), 1)
    firsts = jnp.sum((ends[None, :] <= block_low[:, None]).astype(jnp.int32), 1)
    slot_iota = jnp.arange(MAXIMG, dtype=jnp.int32)
    wanted = jnp.minimum(firsts[:, None] + slot_iota[None, :], images - 1)
    live = slot_iota[None, :] < counts[:, None]
    holders = image_owner[wanted]
    pieces = lax.all_to_all(latents, "ctx", split_axis=2, concat_axis=0, tiled=True)
    outgoing = jnp.where(live[:, :, None, None], pieces[holders], jnp.zeros((), jnp.bfloat16))
    panels = lax.all_to_all(outgoing, "ctx", split_axis=0, concat_axis=3, tiled=True)
    gathered = lax.all_gather(kv_weight, "ctx", axis=0, tiled=True)
    flat_weight = gathered.reshape(gathered.shape[0], 2 * width)
    both = jnp.dot(
        panels.reshape(MAXIMG * lat, panels.shape[3]),
        flat_weight,
        preferred_element_type=jnp.float32,
    )
    keys_out = head_norm(both[:, :width], DH).astype(jnp.bfloat16)
    values_out = both[:, width:].astype(jnp.bfloat16)
    mine = lax.axis_index("ctx")
    positions = mine * tok + jnp.arange(tok, dtype=jnp.int32)
    inside = (positions[:, None] >= starts[None, :]) & (positions[:, None] < ends[None, :])
    has_image = jnp.any(inside, 1)
    which = jnp.sum(jnp.where(inside, jnp.arange(images, dtype=jnp.int32)[None, :], 0), 1)
    my_first = jnp.sum((ends <= mine * tok).astype(jnp.int32))
    slot = which - my_first
    heads_here = width // DH
    query_heads = query_norm.reshape(tok, heads_here, DH)
    key_heads = keys_out.reshape(MAXIMG * lat, heads_here, DH)
    value_heads = values_out.reshape(MAXIMG * lat, heads_here, DH)
    scores = jnp.einsum(
        "thd,khd->thk", query_heads, key_heads, preferred_element_type=jnp.float32
    ) * DH ** (-0.5)
    owner_slot = jnp.arange(MAXIMG * lat, dtype=jnp.int32) // lat
    selected = (has_image[:, None] & (owner_slot[None, :] == slot[:, None])).astype(jnp.float32)
    weighted = jnp.exp(scores) * selected[:, None, :]
    total = (
        jnp.sum(weighted, -1, keepdims=True) + (1.0 - has_image.astype(jnp.float32))[:, None, None]
    )
    probs = (weighted / total).astype(jnp.bfloat16)
    attended = jnp.einsum("thk,khd->thd", probs, value_heads, preferred_element_type=jnp.float32)
    attended = attended.reshape(tok, width)
    gated = (jnp.tanh(attn_gate)[None, :] * attended).astype(jnp.bfloat16)
    return lax.all_to_all(gated, "head", split_axis=0, concat_axis=1, tiled=True)


def shards(*args):
    ctx_count = lax.axis_size("ctx")
    weight = args[4]
    pairs = lax.axis_size("groups") == 2 and lax.axis_size("head") == 2
    whole_heads = weight.shape[2] == 2 * ctx_count * DH
    whole_blocks = ctx_count == 8 and args[1].shape[2] % (2 * DH) == 0 and args[1].shape[2] > 6 * DH and weight.shape[0] % 32 == 0
    if pairs and whole_heads and whole_blocks and ctx_count & (ctx_count - 1) == 0:
        return by_heads(*args)
    return by_tokens(*args)


def solution(mesh):
    placed = (
        P(("groups", "ctx", "head"), None),
        P(("groups", "ctx"), None, None),
        P("groups", None),
        P("groups"),
        P("ctx", None, "head"),
        P("head"),
    )
    return jax.shard_map(
        shards,
        mesh=mesh,
        in_specs=placed,
        out_specs=P(("groups", "ctx", "head"), None),
        check_vma=False,
    )
```
